32 devices in a mesh: head: 4 (over z), seq: 4 (over x, core), req: 2 (over y).
Axes of the slice: x: 2, y: 2, z: 4, core: 2. Of those that a mesh axis runs over, the one named last changes fastest.
Arguments:
- stream: bfloat16 [1024, 2048], P(('req', 'seq', 'head')), may hold values from -12 to 12
- queries: bfloat16 [1024, 4096], P(('req', 'seq'), 'head'), may hold values from -16 to 16
- cache_pairs: bfloat16 [1024, 4, 128, 256], P(('req', 'seq'), 'head'), may hold values from -16 to 16
- fresh_pairs: bfloat16 [1024, 4, 256], P(('req', 'seq'), 'head'), may hold values from -16 to 16
- kept_slots: int32 [1024, 4, 96], P(('req', 'seq'), 'head'), may hold values from 0 to 31, as said below
- segment_kept_count: int32 [1024, 4, 4], P(('req', 'seq'), 'head'), may hold values from 1 to 24, 60 in all within a row
- output_weight: bfloat16 [4096, 2048], P('head', 'seq'), may hold values from -0.09375 to 0.09375
- norm_gain: float32 [2048], replicated, may hold values from 0.1 to 1.9
- routes: int32 [1024, 8], P(('req', 'seq', 'head')), may hold values from 0 to 7, all different within a row; in each aligned block of 32 rows (0 to 31, 32 to 63, ...) at most 32 rows name the same one
- gate_codes: int32 [1024, 8], P(('req', 'seq', 'head')), may hold values from 1 to 16
- gate_weight: bfloat16 [8, 2048, 768], P(('seq', 'req')), may hold values from -0.125 to 0.125
- up_weight: bfloat16 [8, 2048, 768], P(('seq', 'req')), may hold values from -0.125 to 0.125
- down_weight: bfloat16 [8, 768, 2048], P(('seq', 'req')), may hold values from -0.21875 to 0.21875
Outputs:
- layer_out: bfloat16 [1024, 2048], P(('req', 'seq', 'head'))
The draws below stay inside these ranges and needn't reach their ends.
Inputs may be any that keep to these rules, and one draw needn't show every extreme that they name: `kept_slots`: entries s * 24 to (s + 1) * 24 - 1 of a list are distinct positions within segment s, counted from the segment's start; only the first segment_kept_count[r, h, s] of them are used. `segment_kept_count`: the 4 counts of a request's head add up to 60. `routes`: A token names 8 different experts. In each aligned block of 32 rows (the tokens of one device) no expert is named more than 32 times.
All inputs are finite; a program needn't handle non-finite values.
Results may differ from the reference program's by a relative error of at most 0.01.
Values may be sent and summed in bfloat16 or wider, within the bound.
A program may use at most 128 MiB of HBM per device.

```python
import math
import jax
import jax.numpy as jnp
import numpy as np
from jax import lax

D = 2048
QUERY_HEADS = 32
KEY_VALUE_HEADS = 4
HEAD_WIDTH = 128
FF = 768
TOPK = 8
TOK_DEV = 32
CACHE_SEGMENTS = 4
SEGMENT_LENGTH = 32
SEGMENT_KEPT_MAX = 24
REQUEST_COUNT = 1024
CONTEXT_LENGTH = 128
KEPT_PER_HEAD = 60
E = 8
CAP = 32


def draw_stream(key, part):
    values = jax.random.normal(jax.random.fold_in(key, 11), (REQUEST_COUNT, D), jnp.float32)
    return jnp.clip(values, -12.0, 12.0).astype(jnp.bfloat16)


def draw_queries(key, part):
    query_shape = (REQUEST_COUNT, QUERY_HEADS * HEAD_WIDTH)
    values = 2.0 * jax.random.normal(jax.random.fold_in(key, 21), query_shape, jnp.float32)
    return jnp.clip(values, -16.0, 16.0).astype(jnp.bfloat16)


def raised_index_pairs(key, salt, pair_shape):
    values = jax.random.normal(jax.random.fold_in(key, salt), pair_shape, jnp.float32)
    return jnp.clip(values, -16.0, 16.0).astype(jnp.bfloat16)


def draw_cache_pairs(key, part):
    return raised_index_pairs(key, 31, (REQUEST_COUNT, KEY_VALUE_HEADS, CONTEXT_LENGTH, 2 * HEAD_WIDTH))


def draw_fresh_pairs(key, part):
    return raised_index_pairs(key, 41, (REQUEST_COUNT, KEY_VALUE_HEADS, 2 * HEAD_WIDTH))


def draw_kept_slots(key, part):
    unscaled_scores = jax.random.randint(jax.random.fold_in(key, 51), (REQUEST_COUNT, KEY_VALUE_HEADS, CACHE_SEGMENTS, SEGMENT_LENGTH), 0, 1 << 19)
    distinct = unscaled_scores * SEGMENT_LENGTH + jnp.arange(SEGMENT_LENGTH, dtype=jnp.int32)
    sorted_order = jnp.argsort(distinct, axis=-1)
    return sorted_order[..., :SEGMENT_KEPT_MAX].reshape(REQUEST_COUNT, KEY_VALUE_HEADS, CACHE_SEGMENTS * SEGMENT_KEPT_MAX).astype(jnp.int32)


def place_ends(entries, stream_key, low, high):
    dims = entries.shape
    place = [jax.random.randint(jax.random.fold_in(stream_key, axis), (), 0, dims[axis]) for axis in range(len(dims))]
    entries = entries.at[tuple(place)].set(low)
    longest = dims.index(max(dims))
    place[longest] = (place[longest] + 1) % dims[longest]
    return entries.at[tuple(place)].set(high)


def levels(rng, dims, cuts, low, high):
    gain, own = 1.0, jax.random.fold_in(rng, 6)
    for dim, parts in cuts:
        steps = jnp.exp(jax.random.uniform(jax.random.fold_in(own, dim), (parts,), jnp.float32, low / len(cuts), high / len(cuts)))
        gain = gain * jnp.repeat(steps, dims[dim] // parts).reshape([-1 if axis == dim else 1 for axis in range(len(dims))])
    return gain


def length_profile(number_of, total, bound, skew):
    portions = [(1 << 20) // math.isqrt(standing ** skew) + 1 for standing in range(2, number_of + 1)]
    rest, counts = total - bound - (number_of - 1), [1] * (number_of - 1)
    while rest > 0:
        free = [i for i in range(number_of - 1) if counts[i] < bound]
        pool, remaining = sum([portions[i] for i in free]), rest
        for i in free:
            extra = min(bound - counts[i], max(1, remaining * portions[i] // pool), rest)
            counts[i] = counts[i] + extra
            rest = rest - extra
    return np.array([bound] + counts)


def uneven(stream_key, count, total, most, lean):
    if count == 2:
        one = jax.random.randint(stream_key, (), max(1, total - most), min(most, total - 1) + 1)
        return jnp.stack([one, total - one])
    tallies = jnp.asarray(length_profile(count, total, most, lean), jnp.int32)
    couples = (count - 1) // 2
    source_of, taker = tallies[1:1 + 2 * couples:2], tallies[2:2 + 2 * couples:2]
    margin = jnp.minimum(source_of - 1, most - taker)
    shifted = jax.random.randint(jax.random.fold_in(stream_key, 1), (couples,), 0, 1 << 20) % (margin + 1)
    tallies = tallies.at[1:1 + 2 * couples:2].set(source_of - shifted).at[2:2 + 2 * couples:2].set(taker + shifted)
    return tallies[jax.random.permutation(jax.random.fold_in(stream_key, 2), count)]


def deal_out(key, own, number, rows, amount, top, bound, skew):
    order = jax.random.permutation(key, amount)
    heavy_load, common = load_shares(amount, rows * top, bound, skew, True), load_shares(amount, rows * top, bound, skew, False)
    places = jnp.arange(amount)

    def named(tallies, rotation):
        used = int((tallies > 0).sum())
        fixed = max(1, used // 4)
        moved = fixed + (places - fixed + rotation * (used - fixed)) % max(1, amount - fixed)
        return jnp.zeros((amount,), jnp.int32).at[order[jnp.where(places < fixed, places, moved)]].set(jnp.asarray(tallies, jnp.int32))

    tallies = jnp.where(number % 4 == 0, named(heavy_load, number // 4), named(common, number - number // 4 - 1))
    mixed = jax.random.permutation(jax.random.fold_in(own, 3), amount)
    donor, taker = mixed[0:amount // 2 * 2:2], mixed[1:amount // 2 * 2:2]
    margin = jnp.minimum(tallies[donor] - 1, bound - tallies[taker]) // 2
    margin = jnp.where((donor == order[0]) | (taker == order[0]) | (tallies[taker] == 0), 0, jnp.maximum(margin, 0))
    moved = jax.random.randint(jax.random.fold_in(own, 4), (amount // 2,), 0, 1 << 20) % (margin + 1)
    tallies = tallies.at[donor].add(-moved).at[taker].add(moved)
    labels = jnp.searchsorted(jnp.cumsum(tallies), jnp.arange(rows * top), side="right").astype(jnp.int32)
    table = labels.reshape(top, rows).T
    table = table[jax.random.permutation(jax.random.fold_in(own, 1), rows)]
    rotation = jax.random.randint(jax.random.fold_in(own, 2), (rows, 1), 0, top)
    return jnp.take_along_axis(table, (jnp.arange(top)[None, :] + rotation) % top, axis=1)


def load_shares(number_of, total, reach, slope, full):
    portions = [(1 << 20) // math.isqrt(rank ** slope) + 1 for rank in range(1, number_of + 1)]
    largest = reach if full else min(reach, max(-(-total // number_of), total * portions[0] // sum(portions)))
    least = 1 if total - largest >= number_of - 1 else 0
    given, spare = [largest] + [least] * (number_of - 1), total - largest - least * (number_of - 1)
    while spare > 0:
        candidates = [i for i in range(1, number_of) if given[i] < largest] or [i for i in range(1, number_of) if given[i] < reach]
        whole, remaining = sum([portions[i] for i in candidates]), spare
        for i in candidates:
            extra = min(reach - given[i], max(1, remaining * portions[i] // whole), spare)
            given[i] = given[i] + extra
            spare = spare - extra
    return np.array(given)


def bell_draw(own_key, shape, scale, most, cuts=(), kind=jnp.bfloat16):
    gain = levels(own_key, shape, cuts, -0.22, 0.18) if cuts else 1.0
    entries = jax.random.normal(own_key, shape, jnp.float32) * scale * gain
    return jnp.minimum(jnp.maximum(entries, -most), most).astype(kind)


def setup_inputs(seed: int = 0) -> dict:
    splits = jax.random.split(jax.random.key(seed), 14)
    stream = draw_stream(jax.random.fold_in(splits[13], 71), 0)
    queries = draw_queries(jax.random.fold_in(splits[13], 71), 0)
    cache_pairs = draw_cache_pairs(jax.random.fold_in(splits[13], 71), 0)
    fresh_pairs = draw_fresh_pairs(jax.random.fold_in(splits[13], 71), 0)
    kept_slots = draw_kept_slots(jax.random.fold_in(splits[13], 71), 0)
    segment_kept_count = jax.vmap(lambda own: uneven(own, CACHE_SEGMENTS, KEPT_PER_HEAD, SEGMENT_KEPT_MAX, 2))(jax.random.split(splits[5], REQUEST_COUNT * KEY_VALUE_HEADS)).reshape((REQUEST_COUNT, KEY_VALUE_HEADS, CACHE_SEGMENTS)).astype(jnp.int32)
    output_weight = bell_draw(splits[6], (QUERY_HEADS * HEAD_WIDTH, D), (QUERY_HEADS * HEAD_WIDTH) ** -0.5, 0.09375, ((0, 4), (1, 4)))
    norm_gain = jnp.clip(1.0 + 0.18 * jax.random.normal(splits[7], (D,), jnp.float32), 0.1, 1.9)
    routes_keys = jax.random.split(jax.random.fold_in(splits[8], 1), REQUEST_COUNT // TOK_DEV)
    routes_turns = jax.random.permutation(jax.random.fold_in(splits[8], 3), REQUEST_COUNT // TOK_DEV)
    routes = jax.vmap(lambda own, number: deal_out(jax.random.fold_in(splits[8], 2), own, number, TOK_DEV, E, TOPK, CAP, 2))(routes_keys, routes_turns).reshape((REQUEST_COUNT, TOPK))
    gate_codes = place_ends(jax.random.randint(splits[9], (REQUEST_COUNT, TOPK), 1, 17), jax.random.fold_in(splits[9], 1), 1, 16).astype(jnp.int32)
    gate_weight = bell_draw(splits[10], (E, D, FF), D ** -0.5, 0.125, ((0, 8),))
    up_weight = bell_draw(splits[11], (E, D, FF), D ** -0.5, 0.125, ((0, 8),))
    down_weight = bell_draw(splits[12], (E, FF, D), FF ** -0.5, 0.21875, ((0, 8),))
    return {"stream": stream, "queries": queries, "cache_pairs": cache_pairs, "fresh_pairs": fresh_pairs, "kept_slots": kept_slots, "segment_kept_count": segment_kept_count, "output_weight": output_weight, "norm_gain": norm_gain, "routes": routes, "gate_codes": gate_codes, "gate_weight": gate_weight, "up_weight": up_weight, "down_weight": down_weight}


def attend_one(single_query_row, cache_entry_row, kept_slot_row, count_row, fresh_row):
    query_group_width = QUERY_HEADS // KEY_VALUE_HEADS
    query_matrix = single_query_row.reshape(KEY_VALUE_HEADS, query_group_width, HEAD_WIDTH).astype(jnp.float32)
    segment_starts = (jnp.arange(CACHE_SEGMENTS, dtype=jnp.int32) * SEGMENT_LENGTH)[None, :, None]
    cache_location = (kept_slot_row.reshape(KEY_VALUE_HEADS, CACHE_SEGMENTS, SEGMENT_KEPT_MAX) + segment_starts).astype(jnp.int32)
    selected_entries = jnp.take_along_axis(cache_entry_row, cache_location.reshape(KEY_VALUE_HEADS, CACHE_SEGMENTS * SEGMENT_KEPT_MAX)[:, :, None], axis=1)
    selected_entries = selected_entries.reshape(KEY_VALUE_HEADS, CACHE_SEGMENTS, SEGMENT_KEPT_MAX, 2 * HEAD_WIDTH).astype(jnp.float32)
    key_part = selected_entries[..., :HEAD_WIDTH]
    value_part = selected_entries[..., HEAD_WIDTH:]
    score_scale = HEAD_WIDTH ** (-0.5)
    scores = jnp.einsum('hgd,hskd->hsgk', query_matrix, key_part) * score_scale
    valid_mask = jnp.arange(SEGMENT_KEPT_MAX, dtype=jnp.int32)[None, None, None, :] < count_row[:, :, None, None]
    seg_max = lax.optimization_barrier(jnp.max(jnp.where(valid_mask, scores, -jnp.inf), axis=-1))
    rounded = jnp.where(valid_mask, jnp.exp(scores - seg_max[..., None]), 0.0).astype(jnp.bfloat16)
    soft_probs = lax.optimization_barrier(rounded).astype(jnp.float32)
    seg_sum = lax.optimization_barrier(jnp.sum(soft_probs, axis=-1))
    seg_acc = jnp.einsum('hsgk,hskd->hsgd', soft_probs, value_part)
    top_score = lax.optimization_barrier(jnp.max(seg_max, axis=1))
    factor = jnp.exp(seg_max - top_score[:, None, :])
    denom_sum = lax.optimization_barrier(jnp.sum(factor * seg_sum, axis=1))
    numer_sum = lax.optimization_barrier(jnp.sum(factor[..., None] * seg_acc, axis=1))
    fresh_float = fresh_row.astype(jnp.float32)
    own_score = jnp.einsum('hgd,hd->hg', query_matrix, fresh_float[:, :HEAD_WIDTH]) * score_scale
    new_top = jnp.maximum(top_score, own_score)
    keep_old = jnp.exp(top_score - new_top)
    take_new = jnp.exp(own_score - new_top)
    denom_sum = denom_sum * keep_old + take_new
    numer_sum = numer_sum * keep_old[..., None] + take_new[..., None] * fresh_float[:, None, HEAD_WIDTH:]
    return (numer_sum / denom_sum[..., None]).reshape(QUERY_HEADS * HEAD_WIDTH).astype(jnp.bfloat16)

def reference(stream, queries, cache_pairs, fresh_pairs, kept_slots, segment_kept_count, output_weight, norm_gain, routes, gate_codes, gate_weight, up_weight, down_weight):
    head_out = lax.map(lambda packed: attend_one(*packed), (queries, cache_pairs, kept_slots, segment_kept_count, fresh_pairs))
    attention = jnp.dot(head_out, output_weight, preferred_element_type=jnp.float32)
    residual = (stream.astype(jnp.float32) + attention).astype(jnp.bfloat16)
    widened = residual.astype(jnp.float32)
    normed = (widened * lax.rsqrt(lax.optimization_barrier(jnp.mean(widened * widened, axis=-1, keepdims=True)) + 1e-06) * norm_gain).astype(jnp.bfloat16)
    code_float = gate_codes.astype(jnp.float32)
    weights = code_float / lax.optimization_barrier(jnp.sum(code_float, axis=-1, keepdims=True))
    row_limit = min(REQUEST_COUNT, CAP * (REQUEST_COUNT // TOK_DEV))
    order_score = (REQUEST_COUNT - jnp.arange(REQUEST_COUNT, dtype=jnp.int32)).astype(jnp.int32)

    def expert_step(mixture, packed):
        gate_mat, up_mat, down_mat, expert = packed
        hit_mask = routes == expert
        share_of = lax.optimization_barrier(jnp.sum(jnp.where(hit_mask, weights, 0.0), axis=-1))
        present = jnp.any(hit_mask, axis=-1)
        unused, chosen = lax.top_k(jnp.where(present, order_score, 0).astype(jnp.int32), row_limit)
        selected_entries = normed[chosen]
        gate_val = jnp.dot(selected_entries, gate_mat, preferred_element_type=jnp.float32)
        upward = jnp.dot(selected_entries, up_mat, preferred_element_type=jnp.float32)
        activated = (jax.nn.silu(gate_val) * upward).astype(jnp.bfloat16)
        result = jnp.dot(activated, down_mat, preferred_element_type=jnp.float32)
        mixture = mixture.at[chosen].add(share_of[chosen][:, None] * result)
        return (mixture, None)
    mixture, unused = lax.scan(expert_step, jnp.zeros((REQUEST_COUNT, D), jnp.float32), (gate_weight, up_weight, down_weight, jnp.arange(E, dtype=jnp.int32)))
    return (residual.astype(jnp.float32) + mixture).astype(jnp.bfloat16)
```

```python
import math

import jax
import jax.numpy as jnp
from jax import lax
from jax.experimental import pallas as pl
from jax.experimental.pallas import tpu as pltpu
from jax.sharding import PartitionSpec as P

epsilon = 1e-06


def attend_kernel(query_ref, cache_ref, fresh_ref, slots_ref, count_ref, out_ref, keep, spread, numer):
    step = pl.program_id(0)
    rows, context, pair_width = cache_ref.shape
    width = pair_width // 2
    groups = query_ref.shape[1] // width
    segments = count_ref.shape[0]
    listed = slots_ref.shape[0] // segments
    length = context // segments
    requests = slots_ref.shape[1]

    @pl.when(step == 0)
    def _():
        place = lax.broadcasted_iota(jnp.int32, (length, requests), 0)
        for segment in range(segments):
            count = count_ref[segment : segment + 1, :]
            found = jnp.zeros((length, requests), jnp.float32)
            for entry in range(listed):
                at = segment * listed + entry
                slot = jnp.where(entry < count, slots_ref[at : at + 1, :], -1)
                found = jnp.where(place == slot, 1.0, found)
            keep[:, segment * length : (segment + 1) * length] = found.T

    for group in range(groups):
        spread[pl.ds(group, rows, stride=groups), :] = query_ref[
            :, group * width : (group + 1) * width
        ].astype(jnp.float32)
    query = spread[...]
    query_low = query.astype(jnp.bfloat16)
    scores = []
    for pair in range(rows // 2):
        keys = cache_ref[2 * pair : 2 * pair + 2, :, :width].reshape(2 * context, width)
        both = lax.dot_general(
            query_low[2 * pair * groups : (2 * pair + 2) * groups, :],
            keys,
            (((1,), (1,)), ((), ())),
            preferred_element_type=jnp.float32,
        )
        scores += [both[:groups, :context], both[groups:, context:]]
    scores = jnp.stack(scores) * width ** (-0.5)
    kept = keep[pl.ds(pl.multiple_of(step * rows, rows), rows), :][:, None, :] > 0.0
    fresh = fresh_ref[...].astype(jnp.float32)
    own = (
        jnp.sum(
            query.reshape(rows, groups, width) * fresh[:, None, :width], axis=-1, keepdims=True
        )
        * width ** (-0.5)
    )
    scores = jnp.where(kept, scores, -jnp.inf)
    top = jnp.maximum(jnp.max(scores, axis=-1, keepdims=True), own)
    probs = jnp.exp(scores - top)
    take_new = jnp.exp(own - top)
    denom = jnp.sum(probs, axis=-1, keepdims=True) + take_new
    none = jnp.zeros((groups, context), jnp.float32)
    for pair in range(rows // 2):
        values = cache_ref[2 * pair : 2 * pair + 2, :, width:].reshape(2 * context, width)
        first = jnp.concatenate([probs[2 * pair], none], axis=1)
        second = jnp.concatenate([none, probs[2 * pair + 1]], axis=1)
        numer[2 * pair * groups : (2 * pair + 2) * groups, :] = jnp.dot(
            jnp.concatenate([first, second], axis=0).astype(jnp.bfloat16),
            values,
            preferred_element_type=jnp.float32,
        )
    total = numer[...].reshape(rows, groups, width) + take_new * fresh[:, None, width:]
    numer[...] = (total * (1.0 / denom)).reshape(rows * groups, width)
    for group in range(groups):
        out_ref[:, group * width : (group + 1) * width] = numer[
            pl.ds(group, rows, stride=groups), :
        ].astype(jnp.bfloat16)


def attend(queries, cache, fresh, slots, counts):
    requests, context, pair_width = cache.shape
    width = pair_width // 2
    groups = queries.shape[1] // width
    rows = math.gcd(requests, 16)
    return pl.pallas_call(
        attend_kernel,
        grid=(requests // rows,),
        out_shape=jax.ShapeDtypeStruct(queries.shape, jnp.bfloat16),
        in_specs=[
            pl.BlockSpec((rows, queries.shape[1]), lambda i: (i, 0)),
            pl.BlockSpec((rows, context, pair_width), lambda i: (i, 0, 0)),
            pl.BlockSpec((rows, pair_width), lambda i: (i, 0)),
            pl.BlockSpec(slots.shape, lambda i: (0, 0)),
            pl.BlockSpec(counts.shape, lambda i: (0, 0)),
        ],
        out_specs=pl.BlockSpec((rows, queries.shape[1]), lambda i: (i, 0)),
        scratch_shapes=[
            pltpu.VMEM((requests, context), jnp.float32),
            pltpu.VMEM((rows * groups, width), jnp.float32),
            pltpu.VMEM((rows * groups, width), jnp.float32),
        ],
        compiler_params=pltpu.CompilerParams(vmem_limit_bytes=24 * 1024 * 1024),
        cost_estimate=pl.CostEstimate(
            flops=4 * cache.size * groups, bytes_accessed=2 * cache.size, transcendentals=0
        ),
        name="attend",
    )(queries, cache, fresh, slots, counts)


def on_device(
    stream,
    queries,
    cache_pairs,
    fresh_pairs,
    kept_slots,
    segment_kept_count,
    output_weight,
    norm_gain,
    routes,
    gate_codes,
    gate_weight,
    up_weight,
    down_weight,
):
    req_rows = queries.shape[0]
    head_out = attend(
        queries,
        cache_pairs[:, 0],
        fresh_pairs[:, 0],
        kept_slots[:, 0].T,
        segment_kept_count[:, 0].T,
    )
    partial_value = jnp.dot(
        head_out,
        lax.all_gather(output_weight, "seq", axis=1, tiled=True),
        preferred_element_type=jnp.float32,
    )
    partial_value = partial_value.reshape(1, req_rows, -1)
    summed = lax.psum_scatter(
        partial_value.astype(jnp.bfloat16), "head", scatter_dimension=1, tiled=True
    ).astype(jnp.float32)
    attention = summed.reshape(stream.shape[0], -1)
    residual = (stream.astype(jnp.float32) + attention).astype(jnp.bfloat16)
    widened = residual.astype(jnp.float32)
    normed = (
        widened
        * lax.rsqrt(jnp.mean(widened * widened, axis=-1, keepdims=True) + epsilon)
        * norm_gain
    ).astype(jnp.bfloat16)
    tok_rows = routes.shape[0]
    top_count = routes.shape[1]
    local_experts = gate_weight.shape[0]
    owners = lax.axis_size(("seq", "req"))
    experts_all = local_experts * owners
    capacity = min(tok_rows, max(2, 2 * tok_rows * top_count // experts_all))
    flat_ids = routes.reshape(-1)
    flat_count = flat_ids.shape[0]
    match_bool = flat_ids[:, None] == jnp.arange(experts_all, dtype=jnp.int32)[None, :]
    row_pos = jnp.arange(flat_count, dtype=jnp.int32)
    strictly_before = (row_pos[None, :] < row_pos[:, None]).astype(jnp.bfloat16)
    earlier = jnp.dot(
        strictly_before, match_bool.astype(jnp.bfloat16), preferred_element_type=jnp.float32
    )
    slot_rank = jnp.sum(jnp.where(match_bool, earlier, 0.0), axis=1).astype(jnp.int32)
    target = flat_ids * capacity + slot_rank
    slot_ids = jnp.arange(experts_all * capacity, dtype=jnp.int32)
    placing = (target[None, :] == slot_ids[:, None]).astype(jnp.float32)
    token_place = jnp.sum(
        placing.reshape(experts_all * capacity, tok_rows, top_count), axis=-1
    ).astype(jnp.bfloat16)
    outgoing = jnp.dot(token_place, normed, preferred_element_type=jnp.float32).astype(jnp.bfloat16)
    outgoing = outgoing.reshape(owners, local_experts, capacity, -1)
    arrived = lax.all_to_all(outgoing, ("seq", "req"), split_axis=0, concat_axis=0, tiled=True)
    gate_val = jnp.einsum(
        "sjnd,jdf->sjnf", arrived, gate_weight, preferred_element_type=jnp.float32
    )
    upward = jnp.einsum("sjnd,jdf->sjnf", arrived, up_weight, preferred_element_type=jnp.float32)
    activated = (jax.nn.silu(gate_val) * upward).astype(jnp.bfloat16)
    expert_part = jnp.einsum(
        "sjnf,jfd->sjnd", activated, down_weight, preferred_element_type=jnp.float32
    )
    code_float = gate_codes.astype(jnp.float32)
    weights = (code_float / jnp.sum(code_float, axis=-1, keepdims=True)).reshape(-1)
    mixing = jnp.sum(
        (placing * weights[None, :]).reshape(experts_all * capacity, tok_rows, top_count), axis=-1
    ).T
    returned = lax.all_to_all(
        expert_part.astype(jnp.bfloat16), ("seq", "req"), split_axis=0, concat_axis=0, tiled=True
    ).astype(expert_part.dtype)
    mixture = jnp.dot(
        mixing,
        returned.reshape(experts_all * capacity, -1),
        precision=lax.Precision.HIGHEST,
        preferred_element_type=jnp.float32,
    )
    return (widened + mixture).astype(jnp.bfloat16)


def solution(mesh):
    placed = (
        P(("req", "seq", "head"), None),
        P(("req", "seq"), "head"),
        P(("req", "seq"), "head", None, None),
        P(("req", "seq"), "head", None),
        P(("req", "seq"), "head", None),
        P(("req", "seq"), "head", None),
        P("head", "seq"),
        P(),
        P(("req", "seq", "head"), None),
        P(("req", "seq", "head"), None),
        P(("seq", "req"), None, None),
        P(("seq", "req"), None, None),
        P(("seq", "req"), None, None),
    )
    return jax.shard_map(
        on_device,
        mesh=mesh,
        in_specs=placed,
        out_specs=P(("req", "seq", "head"), None),
        check_vma=False,
    )
```

```python
import math

import jax
import jax.numpy as jnp
from jax import lax
from jax.experimental import pallas as pl
from jax.experimental.pallas import tpu as pltpu
from jax.sharding import PartitionSpec as P

epsilon = 1e-06


def attend_kernel(query_ref, cache_ref, fresh_ref, slots_ref, count_ref, out_ref, keep, spread, numer):
    step = pl.program_id(0)
    rows, context, pair_width = cache_ref.shape
    width = pair_width // 2
    groups = query_ref.shape[1] // width
    segments = count_ref.shape[0]
    listed = slots_ref.shape[0] // segments
    length = context // segments
    requests = slots_ref.shape[1]

    @pl.when(step == 0)
    def _():
        place = lax.broadcasted_iota(jnp.int32, (length, requests), 0)
        for segment in range(segments):
            count = count_ref[segment : segment + 1, :]
            found = jnp.zeros((length, requests), jnp.float32)
            for entry in range(listed):
                at = segment * listed + entry
                slot = jnp.where(entry < count, slots_ref[at : at + 1, :], -1)
                found = jnp.where(place == slot, 1.0, found)
            keep[:, segment * length : (segment + 1) * length] = found.T

    for group in range(groups):
        spread[pl.ds(group, rows, stride=groups), :] = query_ref[
            :, group * width : (group + 1) * width
        ].astype(jnp.float32)
    query = spread[...]
    query_low = query.astype(jnp.bfloat16)
    scores = []
    for pair in range(rows // 2):
        keys = cache_ref[2 * pair : 2 * pair + 2, :, :width].reshape(2 * context, width)
        both = lax.dot_general(
            query_low[2 * pair * groups : (2 * pair + 2) * groups, :],
            keys,
            (((1,), (1,)), ((), ())),
            preferred_element_type=jnp.float32,
        )
        scores += [both[:groups, :context], both[groups:, context:]]
    scores = jnp.stack(scores) * width ** (-0.5)
    kept = keep[pl.ds(pl.multiple_of(step * rows, rows), rows), :][:, None, :] > 0.0
    fresh = fresh_ref[...].astype(jnp.float32)
    own = (
        jnp.sum(
            query.reshape(rows, groups, width) * fresh[:, None, :width], axis=-1, keepdims=True
        )
        * width ** (-0.5)
    )
    scores = jnp.where(kept, scores, -jnp.inf)
    top = jnp.maximum(jnp.max(scores, axis=-1, keepdims=True), own)
    probs = jnp.exp(scores - top)
    take_new = jnp.exp(own - top)
    denom = jnp.sum(probs, axis=-1, keepdims=True) + take_new
    none = jnp.zeros((groups, context), jnp.float32)
    for pair in range(rows // 2):
        values = cache_ref[2 * pair : 2 * pair + 2, :, width:].reshape(2 * context, width)
        first = jnp.concatenate([probs[2 * pair], none], axis=1)
        second = jnp.concatenate([none, probs[2 * pair + 1]], axis=1)
        numer[2 * pair * groups : (2 * pair + 2) * groups, :] = jnp.dot(
            jnp.concatenate([first, second], axis=0).astype(jnp.bfloat16),
            values,
            preferred_element_type=jnp.float32,
        )
    total = numer[...].reshape(rows, groups, width) + take_new * fresh[:, None, width:]
    numer[...] = (total * (1.0 / denom)).reshape(rows * groups, width)
    for group in range(groups):
        out_ref[:, group * width : (group + 1) * width] = numer[
            pl.ds(group, rows, stride=groups), :
        ].astype(jnp.bfloat16)


def attend(queries, cache, fresh, slots, counts):
    requests, context, pair_width = cache.shape
    width = pair_width // 2
    groups = queries.shape[1] // width
    rows = math.gcd(requests, 16)
    return pl.pallas_call(
        attend_kernel,
        grid=(requests // rows,),
        out_shape=jax.ShapeDtypeStruct(queries.shape, jnp.bfloat16),
        in_specs=[
            pl.BlockSpec((rows, queries.shape[1]), lambda i: (i, 0)),
            pl.BlockSpec((rows, context, pair_width), lambda i: (i, 0, 0)),
            pl.BlockSpec((rows, pair_width), lambda i: (i, 0)),
            pl.BlockSpec(slots.shape, lambda i: (0, 0)),
            pl.BlockSpec(counts.shape, lambda i: (0, 0)),
        ],
        out_specs=pl.BlockSpec((rows, queries.shape[1]), lambda i: (i, 0)),
        scratch_shapes=[
            pltpu.VMEM((requests, context), jnp.float32),
            pltpu.VMEM((rows * groups, width), jnp.float32),
            pltpu.VMEM((rows * groups, width), jnp.float32),
        ],
        compiler_params=pltpu.CompilerParams(vmem_limit_bytes=56 * 1024 * 1024),
        cost_estimate=pl.CostEstimate(
            flops=4 * cache.size * groups, bytes_accessed=2 * cache.size, transcendentals=0
        ),
        name="attend",
    )(queries, cache, fresh, slots, counts)


def layer_kernel(
    heads_ref, outw_hbm, stream_ref, gain_ref, routes_ref, codes_ref, gate_hbm, up_hbm, down_hbm,
    out_ref,
    outw, gate, up, down, gathered, partial, terms, attn, tokens, expert,
    twin_out, twin_in, side_out, side_in,
    load_sem, gather_send, gather_recv, term_send, term_recv, token_send, token_recv,
    twin_send, twin_recv, side_send, side_recv,
):
    head, seq, req = lax.axis_index("head"), lax.axis_index("seq"), lax.axis_index("req")
    head_count, seq_count = lax.axis_size("head"), lax.axis_size("seq")
    tok, model = stream_ref.shape
    columns = outw.shape[1]
    twin = seq + 1 - 2 * (seq % 2)
    far = (seq + 2) % seq_count
    seqs = (seq, twin, far, (twin + 2) % seq_count)
    over_twin, over_far, over_req = {"seq": twin}, {"seq": far}, {"req": 1 - req}

    loads = [
        pltpu.make_async_copy(source, target, load_sem.at[i])
        for i, (source, target) in enumerate(
            ((outw_hbm, outw), (gate_hbm, gate), (up_hbm, up), (down_hbm, down))
        )
    ]
    for load in loads:
        load.start()

    def remote(source, target, sends, recvs, index, device):
        copy = pltpu.make_async_remote_copy(
            src_ref=source,
            dst_ref=target,
            send_sem=sends.at[index],
            recv_sem=recvs.at[index],
            device_id=device,
            device_id_type=pl.DeviceIdType.MESH,
        )
        copy.start()
        return copy

    barrier = pltpu.get_barrier_semaphore()
    met = [over_req] + [
        {"head": (head + up_by) % head_count, "seq": seqs[k]}
        for up_by in range(head_count)
        for k in range(4)
        if up_by or k
    ]
    for device in met:
        pl.semaphore_signal(barrier, inc=1, device_id=device, device_id_type=pl.DeviceIdType.MESH)

    lane = lax.broadcasted_iota(jnp.int32, (tok, tokens.shape[2] - model), 1)
    coded = jnp.zeros(lane.shape, jnp.float32)
    for k in range(routes_ref.shape[1]):
        coded = jnp.where(
            routes_ref[:, k : k + 1] == lane, codes_ref[:, k : k + 1].astype(jnp.float32), coded
        )
    tokens[0, :, model:] = coded.astype(jnp.bfloat16)
    pl.semaphore_wait(barrier, len(met))

    half = heads_ref.shape[0] // 2
    parts = [pl.ds(0, half), pl.ds(half, half)]
    to_far = [
        remote(
            heads_ref.at[rows], gathered.at[1, rows], gather_send, gather_recv, 1 + i, over_far
        )
        for i, rows in enumerate(parts)
    ]
    to_twin = remote(heads_ref, gathered.at[0], gather_send, gather_recv, 0, over_twin)
    sent = to_far + [to_twin]
    summed = []

    def project(k, block):
        partial[k] = jnp.dot(block, outw[...], preferred_element_type=jnp.float32).astype(
            jnp.bfloat16
        )
        for up_by in (2, 1, 3, 0):
            if up_by or k:
                target = (head + up_by) % head_count
                rows = pl.ds(pl.multiple_of(target * tok, tok), tok)
                summed.append(
                    remote(
                        partial.at[k, rows],
                        terms.at[up_by, k],
                        term_send,
                        term_recv,
                        4 * up_by + k,
                        {"head": target, "seq": seqs[k]},
                    )
                )

    loads[0].wait()
    project(0, heads_ref[...])
    to_twin.wait_recv()
    project(1, gathered[0])
    passed = []
    for i, rows in enumerate(parts):
        to_far[i].wait_recv()
        passed.append(
            remote(
                gathered.at[1, rows], gathered.at[2, rows], gather_send, gather_recv, 3 + i,
                over_twin,
            )
        )
    project(2, gathered[1])
    for copy in passed:
        copy.wait_recv()
    project(3, gathered[2])
    sent += passed

    for copy in summed:
        copy.wait_recv()
    mine = pl.ds(pl.multiple_of(head * tok, tok), tok)
    for k in range(4):
        total = (partial[0, mine] if k == 0 else terms[0, k]).astype(jnp.float32)
        for up_by in range(1, head_count):
            total = total + terms[up_by, k].astype(jnp.float32)
        attn[:, pl.ds(pl.multiple_of(seqs[k] * columns, columns), columns)] = total
    residual = (stream_ref[...].astype(jnp.float32) + attn[...]).astype(jnp.bfloat16)
    widened = residual.astype(jnp.float32)
    attn[...] = widened
    mean = jnp.mean(widened * widened, axis=-1, keepdims=True)
    tokens[0, :, :model] = (widened * lax.rsqrt(mean + epsilon) * gain_ref[...]).astype(
        jnp.bfloat16
    )

    def spread(source, target, index, device):
        copy = remote(source, target, token_send, token_recv, index, device)
        sent.append(copy)
        return copy

    from_far = spread(tokens.at[0], tokens.at[2], 1, over_far)
    from_req = spread(tokens.at[0], tokens.at[4], 2, over_req)
    from_twin = spread(tokens.at[0], tokens.at[1], 0, over_twin)
    number = seq * lax.axis_size("req") + req

    def run_expert(first, count):
        rows = pl.ds(first * tok, count * tok)
        arrived = tokens[first : first + count].reshape(count * tok, tokens.shape[2])
        value = arrived[:, :model]
        codes = arrived[:, model:].astype(jnp.float32)
        place = lax.broadcasted_iota(jnp.int32, codes.shape, 1)
        weight = jnp.sum(jnp.where(place == number, codes, 0.0), axis=-1, keepdims=True) / jnp.sum(
            codes, axis=-1, keepdims=True
        )
        gate_val = jnp.dot(value, gate[...], preferred_element_type=jnp.float32)
        upward = jnp.dot(value, up[...], preferred_element_type=jnp.float32)
        act = (jax.nn.silu(gate_val) * upward).astype(jnp.bfloat16)
        expert[rows, :] = weight * jnp.dot(act, down[...], preferred_element_type=jnp.float32)

    def to_other_core(slot):
        at = slot // 2
        twin_out[at] = expert[slot * tok : (slot + 1) * tok, :].astype(jnp.bfloat16)
        copy = remote(twin_out.at[at], twin_in.at[at], twin_send, twin_recv, at, over_twin)
        sent.append(copy)
        return copy

    def with_other_core(slot, copy):
        copy.wait_recv()
        return expert[slot * tok : (slot + 1) * tok, :] + twin_in[slot // 2].astype(jnp.float32)

    def aside(index, value, device):
        side_out[index] = value.astype(jnp.bfloat16)
        copy = remote(
            side_out.at[index], side_in.at[index], side_send, side_recv, index, device
        )
        sent.append(copy)
        return copy

    from_twin.wait_recv()
    loads[1].wait()
    loads[2].wait()
    loads[3].wait()
    run_expert(0, 2)
    pair = tok // 2
    low, high = pl.ds(0, pair), pl.ds(pair, pair)
    from_far.wait_recv()
    corner = [spread(tokens.at[2, low], tokens.at[6, low], 5, over_req)]
    far_twin = spread(tokens.at[2], tokens.at[3], 3, over_twin)
    from_req.wait_recv()
    corner.append(spread(tokens.at[4, high], tokens.at[6, high], 6, over_far))
    req_twin = spread(tokens.at[4], tokens.at[5], 4, over_twin)
    own_copy = to_other_core(1)
    far_twin.wait_recv()
    req_twin.wait_recv()
    run_expert(2, 4)
    far_copy, req_copy = to_other_core(3), to_other_core(5)
    corner_twin = []
    for i, rows in enumerate((low, high)):
        corner[i].wait_recv()
        corner_twin.append(spread(tokens.at[6, rows], tokens.at[7, rows], 7 + i, over_twin))
    middle = model // 2
    far_sum = with_other_core(2, far_copy)
    far_low = aside(0, far_sum[:, :middle], over_far)
    req_sum = with_other_core(4, req_copy)
    req_high = aside(1, req_sum[:, middle:], over_req)
    for copy in corner_twin:
        copy.wait_recv()
    run_expert(6, 2)
    corner_copy = to_other_core(7)
    own_sum = with_other_core(0, own_copy)
    corner_sum = with_other_core(6, corner_copy)
    corner_low = aside(2, corner_sum[:, :middle], over_far)
    corner_high = aside(3, corner_sum[:, middle:], over_req)

    def landed(index, copy):
        copy.wait_recv()
        return side_in[index].astype(jnp.float32)

    last_low = aside(4, req_sum[:, :middle] + landed(2, corner_low), over_req)
    last_high = aside(5, far_sum[:, middle:] + landed(3, corner_high), over_far)
    mixed_low = own_sum[:, :middle] + landed(0, far_low)
    mixed_high = own_sum[:, middle:] + landed(1, req_high)
    out_ref[:, :middle] = (attn[:, :middle] + mixed_low + landed(4, last_low)).astype(jnp.bfloat16)
    out_ref[:, middle:] = (attn[:, middle:] + mixed_high + landed(5, last_high)).astype(
        jnp.bfloat16
    )
    for copy in sent + summed:
        copy.wait_send()


def finish_layer(heads, outw, stream, gain, routes, codes, gate, up, down):
    tok, model = stream.shape
    head_count = lax.axis_size("head")
    members = lax.axis_size("seq") * lax.axis_size("req")
    low, dma = jnp.bfloat16, pltpu.SemaphoreType.DMA
    vmem, anywhere = pl.BlockSpec(memory_space=pltpu.VMEM), pl.BlockSpec(memory_space=pl.ANY)
    return pl.pallas_call(
        layer_kernel,
        out_shape=jax.ShapeDtypeStruct(stream.shape, stream.dtype),
        in_specs=[vmem, anywhere, vmem, vmem, vmem, vmem, anywhere, anywhere, anywhere],
        out_specs=vmem,
        scratch_shapes=[
            pltpu.VMEM(outw.shape, low),
            pltpu.VMEM(gate.shape, low),
            pltpu.VMEM(up.shape, low),
            pltpu.VMEM(down.shape, low),
            pltpu.VMEM((3, *heads.shape), low),
            pltpu.VMEM((4, heads.shape[0], outw.shape[1]), low),
            pltpu.VMEM((head_count, 4, tok, outw.shape[1]), low),
            pltpu.VMEM((tok, model), jnp.float32),
            pltpu.VMEM((members, tok, model + 128), low),
            pltpu.VMEM((members * tok, model), jnp.float32),
            pltpu.VMEM((4, tok, model), low),
            pltpu.VMEM((4, tok, model), low),
            pltpu.VMEM((6, tok, model // 2), low),
            pltpu.VMEM((6, tok, model // 2), low),
            dma((4,)),
            dma((5,)),
            dma((5,)),
            dma((4 * head_count,)),
            dma((4 * head_count,)),
            dma((9,)),
            dma((9,)),
            dma((4,)),
            dma((4,)),
            dma((6,)),
            dma((6,)),
        ],
        compiler_params=pltpu.CompilerParams(
            collective_id=0, has_side_effects=True, vmem_limit_bytes=48 * 1024 * 1024
        ),
        name="finish_layer",
    )(heads, outw, stream, gain, routes, codes, gate, up, down)


def on_device(
    stream,
    queries,
    cache_pairs,
    fresh_pairs,
    kept_slots,
    segment_kept_count,
    output_weight,
    norm_gain,
    routes,
    gate_codes,
    gate_weight,
    up_weight,
    down_weight,
):
    req_rows = queries.shape[0]
    head_out = attend(
        queries,
        cache_pairs[:, 0],
        fresh_pairs[:, 0],
        kept_slots[:, 0].T,
        segment_kept_count[:, 0].T,
    )
    experts_all = gate_weight.shape[0] * lax.axis_size(("seq", "req"))
    if (
        lax.axis_size("seq") == 4
        and lax.axis_size("req") == 2
        and gate_weight.shape[0] == 1
        and routes.shape[1] == experts_all
        and stream.shape[0] % 32 == 0
        and stream.shape[1] % 256 == 0
    ):
        return finish_layer(
            head_out,
            output_weight,
            stream,
            norm_gain[None],
            routes,
            gate_codes,
            gate_weight[0],
            up_weight[0],
            down_weight[0],
        )
    partial_value = jnp.dot(
        head_out,
        lax.all_gather(output_weight, "seq", axis=1, tiled=True),
        preferred_element_type=jnp.float32,
    )
    partial_value = partial_value.reshape(1, req_rows, -1)
    summed = lax.psum_scatter(
        partial_value.astype(jnp.bfloat16), "head", scatter_dimension=1, tiled=True
    ).astype(jnp.float32)
    attention = summed.reshape(stream.shape[0], -1)
    residual = (stream.astype(jnp.float32) + attention).astype(jnp.bfloat16)
    widened = residual.astype(jnp.float32)
    normed = (
        widened
        * lax.rsqrt(jnp.mean(widened * widened, axis=-1, keepdims=True) + epsilon)
        * norm_gain
    ).astype(jnp.bfloat16)
    tok_rows = routes.shape[0]
    top_count = routes.shape[1]
    local_experts = gate_weight.shape[0]
    owners = lax.axis_size(("seq", "req"))
    experts_all = local_experts * owners
    capacity = min(tok_rows, max(2, 2 * tok_rows * top_count // experts_all))
    flat_ids = routes.reshape(-1)
    flat_count = flat_ids.shape[0]
    match_bool = flat_ids[:, None] == jnp.arange(experts_all, dtype=jnp.int32)[None, :]
    row_pos = jnp.arange(flat_count, dtype=jnp.int32)
    strictly_before = (row_pos[None, :] < row_pos[:, None]).astype(jnp.bfloat16)
    earlier = jnp.dot(
        strictly_before, match_bool.astype(jnp.bfloat16), preferred_element_type=jnp.float32
    )
    slot_rank = jnp.sum(jnp.where(match_bool, earlier, 0.0), axis=1).astype(jnp.int32)
    target = flat_ids * capacity + slot_rank
    slot_ids = jnp.arange(experts_all * capacity, dtype=jnp.int32)
    placing = (target[None, :] == slot_ids[:, None]).astype(jnp.float32)
    token_place = jnp.sum(
        placing.reshape(experts_all * capacity, tok_rows, top_count), axis=-1
    ).astype(jnp.bfloat16)
    outgoing = jnp.dot(token_place, normed, preferred_element_type=jnp.float32).astype(jnp.bfloat16)
    outgoing = outgoing.reshape(owners, local_experts, capacity, -1)
    arrived = lax.all_to_all(outgoing, ("seq", "req"), split_axis=0, concat_axis=0, tiled=True)
    gate_val = jnp.einsum(
        "sjnd,jdf->sjnf", arrived, gate_weight, preferred_element_type=jnp.float32
    )
    upward = jnp.einsum("sjnd,jdf->sjnf", arrived, up_weight, preferred_element_type=jnp.float32)
    activated = (jax.nn.silu(gate_val) * upward).astype(jnp.bfloat16)
    expert_part = jnp.einsum(
        "sjnf,jfd->sjnd", activated, down_weight, preferred_element_type=jnp.float32
    )
    code_float = gate_codes.astype(jnp.float32)
    weights = (code_float / jnp.sum(code_float, axis=-1, keepdims=True)).reshape(-1)
    mixing = jnp.sum(
        (placing * weights[None, :]).reshape(experts_all * capacity, tok_rows, top_count), axis=-1
    ).T
    returned = lax.all_to_all(
        expert_part.astype(jnp.bfloat16), ("seq", "req"), split_axis=0, concat_axis=0, tiled=True
    ).astype(expert_part.dtype)
    mixture = jnp.dot(
        mixing,
        returned.reshape(experts_all * capacity, -1),
        precision=lax.Precision.HIGHEST,
        preferred_element_type=jnp.float32,
    )
    return (widened + mixture).astype(jnp.bfloat16)


def solution(mesh):
    placed = (
        P(("req", "seq", "head"), None),
        P(("req", "seq"), "head"),
        P(("req", "seq"), "head", None, None),
        P(("req", "seq"), "head", None),
        P(("req", "seq"), "head", None),
        P(("req", "seq"), "head", None),
        P("head", "seq"),
        P(),
        P(("req", "seq", "head"), None),
        P(("req", "seq", "head"), None),
        P(("seq", "req"), None, None),
        P(("seq", "req"), None, None),
        P(("seq", "req"), None, None),
    )
    return jax.shard_map(
        on_device,
        mesh=mesh,
        in_specs=placed,
        out_specs=P(("req", "seq", "head"), None),
        check_vma=False,
    )
```

```python
import math

import jax
import jax.numpy as jnp
from jax import lax
from jax.experimental import pallas as pl
from jax.experimental.pallas import tpu as pltpu
from jax.sharding import PartitionSpec as P

epsilon = 1e-06


def find_kept(slots_ref, count_ref, keep):
    segments, requests = count_ref.shape
    listed = slots_ref.shape[0] // segments
    length = keep.shape[1] // segments
    place = lax.broadcasted_iota(jnp.int32, (length, requests), 0)
    for segment in range(segments):
        count = count_ref[segment : segment + 1, :]
        found = jnp.zeros((length, requests), jnp.float32)
        for entry in range(listed):
            at = segment * listed + entry
            slot = jnp.where(entry < count, slots_ref[at : at + 1, :], -1)
            found = jnp.where(place == slot, 1.0, found)
        keep[:, segment * length : (segment + 1) * length] = found.T


def attend_rows(rows_at, first, rows, query_ref, cache_ref, fresh_ref, keep, out_ref, spread, numer):
    context, pair_width = cache_ref.shape[1:]
    width = pair_width // 2
    groups = query_ref.shape[1] // width
    for group in range(groups):
        spread[pl.ds(group, rows, stride=groups), :] = query_ref[
            rows_at, group * width : (group + 1) * width
        ].astype(jnp.float32)
    query = spread[...]
    query_low = query.astype(jnp.bfloat16)
    scores = []
    for pair in range(rows // 2):
        keys = cache_ref[pl.ds(first + 2 * pair, 2), :, :width].reshape(2 * context, width)
        both = lax.dot_general(
            query_low[2 * pair * groups : (2 * pair + 2) * groups, :],
            keys,
            (((1,), (1,)), ((), ())),
            preferred_element_type=jnp.float32,
        )
        scores += [both[:groups, :context], both[groups:, context:]]
    scores = jnp.stack(scores) * width ** (-0.5)
    kept = keep[rows_at, :][:, None, :] > 0.0
    fresh = fresh_ref[rows_at, :].astype(jnp.float32)
    own = (
        jnp.sum(
            query.reshape(rows, groups, width) * fresh[:, None, :width], axis=-1, keepdims=True
        )
        * width ** (-0.5)
    )
    scores = jnp.where(kept, scores, -jnp.inf)
    top = jnp.maximum(jnp.max(scores, axis=-1, keepdims=True), own)
    probs = jnp.exp(scores - top)
    take_new = jnp.exp(own - top)
    denom = jnp.sum(probs, axis=-1, keepdims=True) + take_new
    none = jnp.zeros((groups, context), jnp.float32)
    for pair in range(rows // 2):
        values = cache_ref[pl.ds(first + 2 * pair, 2), :, width:].reshape(2 * context, width)
        upper = jnp.concatenate([probs[2 * pair], none], axis=1)
        lower = jnp.concatenate([none, probs[2 * pair + 1]], axis=1)
        numer[2 * pair * groups : (2 * pair + 2) * groups, :] = jnp.dot(
            jnp.concatenate([upper, lower], axis=0).astype(jnp.bfloat16),
            values,
            preferred_element_type=jnp.float32,
        )
    total = numer[...].reshape(rows, groups, width) + take_new * fresh[:, None, width:]
    numer[...] = (total * (1.0 / denom)).reshape(rows * groups, width)
    for group in range(groups):
        out_ref[:, group * width : (group + 1) * width] = numer[
            pl.ds(group, rows, stride=groups), :
        ].astype(jnp.bfloat16)


def attend_kernel(query_ref, cache_ref, fresh_ref, slots_ref, count_ref, out_ref, keep, spread, numer):
    step = pl.program_id(0)
    rows = cache_ref.shape[0]

    @pl.when(step == 0)
    def _():
        find_kept(slots_ref, count_ref, keep)

    at = pl.ds(pl.multiple_of(step * rows, rows), rows)
    own_keep = keep.at[at]
    attend_rows(
        pl.ds(0, rows), 0, rows, query_ref, cache_ref, fresh_ref, own_keep, out_ref, spread, numer
    )


def attend(queries, cache, fresh, slots, counts):
    requests, context, pair_width = cache.shape
    width = pair_width // 2
    groups = queries.shape[1] // width
    rows = math.gcd(requests, 16)
    return pl.pallas_call(
        attend_kernel,
        grid=(requests // rows,),
        out_shape=jax.ShapeDtypeStruct(queries.shape, jnp.bfloat16),
        in_specs=[
            pl.BlockSpec((rows, queries.shape[1]), lambda i: (i, 0)),
            pl.BlockSpec((rows, context, pair_width), lambda i: (i, 0, 0)),
            pl.BlockSpec((rows, pair_width), lambda i: (i, 0)),
            pl.BlockSpec(slots.shape, lambda i: (0, 0)),
            pl.BlockSpec(counts.shape, lambda i: (0, 0)),
        ],
        out_specs=pl.BlockSpec((rows, queries.shape[1]), lambda i: (i, 0)),
        scratch_shapes=[
            pltpu.VMEM((requests, context), jnp.float32),
            pltpu.VMEM((rows * groups, width), jnp.float32),
            pltpu.VMEM((rows * groups, width), jnp.float32),
        ],
        compiler_params=pltpu.CompilerParams(vmem_limit_bytes=56 * 1024 * 1024),
        cost_estimate=pl.CostEstimate(
            flops=4 * cache.size * groups, bytes_accessed=2 * cache.size, transcendentals=0
        ),
        name="attend",
    )(queries, cache, fresh, slots, counts)


def layer_kernel(
    query_hbm, cache_hbm, fresh_hbm, slots_hbm, count_hbm, outw_hbm, stream_hbm, gain_hbm,
    routes_hbm, codes_hbm, gate_hbm, up_hbm, down_hbm,
    out_ref,
    query_ref, cache_ref, fresh_ref, slots_ref, count_ref, outw, stream_ref, gain_ref,
    routes_ref, codes_ref, gate, up, down,
    keep, spread_rows, numer, heads, gathered, partial, terms, attn, tokens, expert,
    twin_out, twin_in, side_out, side_in,
    load_sem, cache_sem, gather_send, gather_recv, term_send, term_recv, token_send, token_recv,
    twin_send, twin_recv, side_send, side_recv,
):
    head, seq, req = lax.axis_index("head"), lax.axis_index("seq"), lax.axis_index("req")
    head_count, seq_count = lax.axis_size("head"), lax.axis_size("seq")
    tok, model = stream_ref.shape
    columns = outw.shape[1]
    twin = seq + 1 - 2 * (seq % 2)
    far = (seq + 2) % seq_count
    seqs = (seq, twin, far, (twin + 2) % seq_count)
    over_twin, over_far, over_req = {"seq": twin}, {"seq": far}, {"req": 1 - req}

    def load(index, source, target):
        copy = pltpu.make_async_copy(source, target, load_sem.at[index])
        copy.start()
        return copy

    attend_loads = [
        load(0, slots_hbm, slots_ref),
        load(1, count_hbm, count_ref),
        load(2, query_hbm, query_ref),
        load(3, fresh_hbm, fresh_ref),
    ]

    def cache_load(index):
        first = lax.rem(head + 1 + index, head_count) * tok
        rows = pl.ds(pl.multiple_of(first, tok), tok)
        return pltpu.make_async_copy(
            cache_hbm.at[rows], cache_ref.at[rows], cache_sem.at[index]
        )

    for index in range(head_count):
        cache_load(index).start()
    route_loads = [load(4, routes_hbm, routes_ref), load(5, codes_hbm, codes_ref)]
    outw_load = load(6, outw_hbm, outw)
    stream_loads = [load(7, stream_hbm, stream_ref), load(8, gain_hbm, gain_ref)]
    expert_loads = [load(9, gate_hbm, gate), load(10, up_hbm, up), load(11, down_hbm, down)]

    def remote(source, target, sends, recvs, index, device):
        copy = pltpu.make_async_remote_copy(
            src_ref=source,
            dst_ref=target,
            send_sem=sends.at[index],
            recv_sem=recvs.at[index],
            device_id=device,
            device_id_type=pl.DeviceIdType.MESH,
        )
        copy.start()
        return copy

    barrier = pltpu.get_barrier_semaphore()
    met = [over_req] + [
        {"head": (head + up_by) % head_count, "seq": seqs[k]}
        for up_by in range(head_count)
        for k in range(4)
        if up_by or k
    ]
    for device in met:
        pl.semaphore_signal(barrier, inc=1, device_id=device, device_id_type=pl.DeviceIdType.MESH)

    for copy in attend_loads[:2]:
        copy.wait()
    find_kept(slots_ref, count_ref, keep)
    for copy in attend_loads[2:] + route_loads:
        copy.wait()
    lanes = tokens.shape[2] - model
    number_at = lax.broadcasted_iota(jnp.int32, (lanes, tok), 0)
    coded = jnp.zeros(number_at.shape, jnp.float32)
    for k in range(routes_ref.shape[0]):
        coded = jnp.where(
            routes_ref[k : k + 1, :] == number_at,
            codes_ref[k : k + 1, :].astype(jnp.float32),
            coded,
        )
    tokens[0, :, model:] = coded.T.astype(jnp.bfloat16)

    def attend_group(index, carry):
        cache_load(index).wait()
        first = pl.multiple_of(lax.rem(head + 1 + index, head_count) * tok, tok)
        attend_rows(
            pl.ds(first, tok), first, tok, query_ref, cache_ref, fresh_ref, keep,
            heads.at[index], spread_rows, numer,
        )
        return carry

    half = head_count // 2
    parts = [slice(0, half), slice(half, head_count)]
    sent, summed, to_far, to_twin = [], [], [], []

    def project(k, source, part):
        block = source[part].reshape(-1, source.shape[2])
        total = jnp.dot(block, outw[...], preferred_element_type=jnp.float32)
        partial[k, part] = total.astype(jnp.bfloat16).reshape(-1, tok, columns)
        for index in range(part.start, part.stop):
            up_by = (index + 1) % head_count
            if up_by or k:
                summed.append(
                    remote(
                        partial.at[k, index],
                        terms.at[up_by, k],
                        term_send,
                        term_recv,
                        4 * up_by + k,
                        {"head": lax.rem(head + up_by, head_count), "seq": seqs[k]},
                    )
                )

    for i, part in enumerate(parts):
        lax.fori_loop(part.start, part.stop, attend_group, 0)
        if i == 0:
            pl.semaphore_wait(barrier, len(met))
            outw_load.wait()
        block = pl.ds(part.start, half)
        to_far.append(
            remote(
                heads.at[block], gathered.at[1, block], gather_send, gather_recv, i, over_far
            )
        )
        to_twin.append(
            remote(
                heads.at[block], gathered.at[0, block], gather_send, gather_recv, 2 + i, over_twin
            )
        )
        project(0, heads, part)
    for copy in to_twin:
        copy.wait_recv()
    project(1, gathered.at[0], slice(0, head_count))
    passed = []
    for i, part in enumerate(parts):
        to_far[i].wait_recv()
        block = pl.ds(part.start, half)
        passed.append(
            remote(
                gathered.at[1, block], gathered.at[2, block], gather_send, gather_recv, 4 + i,
                over_twin,
            )
        )
    project(2, gathered.at[1], slice(0, head_count))
    for copy in passed:
        copy.wait_recv()
    project(3, gathered.at[2], slice(0, head_count))
    sent += to_far + to_twin + passed

    for copy in summed:
        copy.wait_recv()
    for copy in stream_loads:
        copy.wait()
    for k in range(4):
        total = (partial[0, head_count - 1] if k == 0 else terms[0, k]).astype(jnp.float32)
        for up_by in range(1, head_count):
            total = total + terms[up_by, k].astype(jnp.float32)
        attn[:, pl.ds(pl.multiple_of(seqs[k] * columns, columns), columns)] = total
    residual = (stream_ref[...].astype(jnp.float32) + attn[...]).astype(jnp.bfloat16)
    widened = residual.astype(jnp.float32)
    attn[...] = widened
    mean = jnp.mean(widened * widened, axis=-1, keepdims=True)
    tokens[0, :, :model] = (widened * lax.rsqrt(mean + epsilon) * gain_ref[...]).astype(
        jnp.bfloat16
    )

    def spread(source, target, index, device):
        copy = remote(source, target, token_send, token_recv, index, device)
        sent.append(copy)
        return copy

    from_far = spread(tokens.at[0], tokens.at[2], 1, over_far)
    from_req = spread(tokens.at[0], tokens.at[4], 2, over_req)
    from_twin = spread(tokens.at[0], tokens.at[1], 0, over_twin)
    number = seq * lax.axis_size("req") + req

    def run_expert(first, count):
        rows = pl.ds(first * tok, count * tok)
        arrived = tokens[first : first + count].reshape(count * tok, tokens.shape[2])
        value = arrived[:, :model]
        codes = arrived[:, model:].astype(jnp.float32)
        place = lax.broadcasted_iota(jnp.int32, codes.shape, 1)
        weight = jnp.sum(jnp.where(place == number, codes, 0.0), axis=-1, keepdims=True) / jnp.sum(
            codes, axis=-1, keepdims=True
        )
        gate_val = jnp.dot(value, gate[...], preferred_element_type=jnp.float32)
        upward = jnp.dot(value, up[...], preferred_element_type=jnp.float32)
        act = (jax.nn.silu(gate_val) * upward).astype(jnp.bfloat16)
        expert[rows, :] = weight * jnp.dot(act, down[...], preferred_element_type=jnp.float32)

    def to_other_core(slot):
        at = slot // 2
        twin_out[at] = expert[slot * tok : (slot + 1) * tok, :].astype(jnp.bfloat16)
        copy = remote(twin_out.at[at], twin_in.at[at], twin_send, twin_recv, at, over_twin)
        sent.append(copy)
        return copy

    def with_other_core(slot, copy):
        copy.wait_recv()
        return expert[slot * tok : (slot + 1) * tok, :] + twin_in[slot // 2].astype(jnp.float32)

    def aside(index, value, device):
        side_out[index] = value.astype(jnp.bfloat16)
        copy = remote(
            side_out.at[index], side_in.at[index], side_send, side_recv, index, device
        )
        sent.append(copy)
        return copy

    from_twin.wait_recv()
    for copy in expert_loads:
        copy.wait()
    run_expert(0, 2)
    pair = tok // 2
    low, high = pl.ds(0, pair), pl.ds(pair, pair)
    from_far.wait_recv()
    corner = [spread(tokens.at[2, low], tokens.at[6, low], 5, over_req)]
    far_twin = spread(tokens.at[2], tokens.at[3], 3, over_twin)
    from_req.wait_recv()
    corner.append(spread(tokens.at[4, high], tokens.at[6, high], 6, over_far))
    req_twin = spread(tokens.at[4], tokens.at[5], 4, over_twin)
    own_copy = to_other_core(1)
    far_twin.wait_recv()
    req_twin.wait_recv()
    run_expert(2, 4)
    far_copy, req_copy = to_other_core(3), to_other_core(5)
    corner_twin = []
    for i, rows in enumerate((low, high)):
        corner[i].wait_recv()
        corner_twin.append(spread(tokens.at[6, rows], tokens.at[7, rows], 7 + i, over_twin))
    middle = model // 2
    far_sum = with_other_core(2, far_copy)
    far_low = aside(0, far_sum[:, :middle], over_far)
    req_sum = with_other_core(4, req_copy)
    req_high = aside(1, req_sum[:, middle:], over_req)
    for copy in corner_twin:
        copy.wait_recv()
    run_expert(6, 2)
    corner_copy = to_other_core(7)
    own_sum = with_other_core(0, own_copy)
    corner_sum = with_other_core(6, corner_copy)
    corner_low = aside(2, corner_sum[:, :middle], over_far)
    corner_high = aside(3, corner_sum[:, middle:], over_req)

    def landed(index, copy):
        copy.wait_recv()
        return side_in[index].astype(jnp.float32)

    last_low = aside(4, req_sum[:, :middle] + landed(2, corner_low), over_req)
    last_high = aside(5, far_sum[:, middle:] + landed(3, corner_high), over_far)
    mixed_low = own_sum[:, :middle] + landed(0, far_low)
    mixed_high = own_sum[:, middle:] + landed(1, req_high)
    out_ref[:, :middle] = (attn[:, :middle] + mixed_low + landed(4, last_low)).astype(jnp.bfloat16)
    out_ref[:, middle:] = (attn[:, middle:] + mixed_high + landed(5, last_high)).astype(
        jnp.bfloat16
    )
    for copy in sent + summed:
        copy.wait_send()


def whole_layer(queries, cache, fresh, slots, counts, outw, stream, gain, routes, codes, gate, up, down):
    tok, model = stream.shape
    requests, context, pair_width = cache.shape
    width = pair_width // 2
    groups = queries.shape[1] // width
    head_count = lax.axis_size("head")
    members = lax.axis_size("seq") * lax.axis_size("req")
    low, dma = jnp.bfloat16, pltpu.SemaphoreType.DMA
    operands = (
        queries, cache, fresh, slots, counts, outw, stream, gain, routes, codes, gate, up, down
    )
    return pl.pallas_call(
        layer_kernel,
        out_shape=jax.ShapeDtypeStruct(stream.shape, stream.dtype),
        in_specs=[pl.BlockSpec(memory_space=pl.ANY)] * len(operands),
        out_specs=pl.BlockSpec(memory_space=pltpu.VMEM),
        scratch_shapes=[
            *[pltpu.VMEM(operand.shape, operand.dtype) for operand in operands],
            pltpu.VMEM((requests, context), jnp.float32),
            pltpu.VMEM((tok * groups, width), jnp.float32),
            pltpu.VMEM((tok * groups, width), jnp.float32),
            pltpu.VMEM((head_count, tok, queries.shape[1]), low),
            pltpu.VMEM((3, head_count, tok, queries.shape[1]), low),
            pltpu.VMEM((4, head_count, tok, outw.shape[1]), low),
            pltpu.VMEM((head_count, 4, tok, outw.shape[1]), low),
            pltpu.VMEM((tok, model), jnp.float32),
            pltpu.VMEM((members, tok, model + 128), low),
            pltpu.VMEM((members * tok, model), jnp.float32),
            pltpu.VMEM((4, tok, model), low),
            pltpu.VMEM((4, tok, model), low),
            pltpu.VMEM((6, tok, model // 2), low),
            pltpu.VMEM((6, tok, model // 2), low),
            dma((12,)),
            dma((head_count,)),
            dma((6,)),
            dma((6,)),
            dma((4 * head_count,)),
            dma((4 * head_count,)),
            dma((9,)),
            dma((9,)),
            dma((4,)),
            dma((4,)),
            dma((6,)),
            dma((6,)),
        ],
        compiler_params=pltpu.CompilerParams(
            collective_id=0, has_side_effects=True, vmem_limit_bytes=58 * 1024 * 1024
        ),
        name="whole_layer",
    )(*operands)


def on_device(
    stream,
    queries,
    cache_pairs,
    fresh_pairs,
    kept_slots,
    segment_kept_count,
    output_weight,
    norm_gain,
    routes,
    gate_codes,
    gate_weight,
    up_weight,
    down_weight,
):
    req_rows = queries.shape[0]
    cached, fresh = cache_pairs[:, 0], fresh_pairs[:, 0]
    slots, counts = kept_slots[:, 0].T, segment_kept_count[:, 0].T
    experts_all = gate_weight.shape[0] * lax.axis_size(("seq", "req"))
    if (
        lax.axis_size("head") % 2 == 0
        and lax.axis_size("seq") == 4
        and lax.axis_size("req") == 2
        and gate_weight.shape[0] == 1
        and routes.shape[1] == experts_all
        and stream.shape[0] % 32 == 0
        and stream.shape[1] % 256 == 0
    ):
        return whole_layer(
            queries,
            cached,
            fresh,
            slots,
            counts,
            output_weight,
            stream,
            norm_gain[None],
            routes.T,
            gate_codes.T,
            gate_weight[0],
            up_weight[0],
            down_weight[0],
        )
    head_out = attend(queries, cached, fresh, slots, counts)
    partial_value = jnp.dot(
        head_out,
        lax.all_gather(output_weight, "seq", axis=1, tiled=True),
        preferred_element_type=jnp.float32,
    )
    partial_value = partial_value.reshape(1, req_rows, -1)
    summed = lax.psum_scatter(
        partial_value.astype(jnp.bfloat16), "head", scatter_dimension=1, tiled=True
    ).astype(jnp.float32)
    attention = summed.reshape(stream.shape[0], -1)
    residual = (stream.astype(jnp.float32) + attention).astype(jnp.bfloat16)
    widened = residual.astype(jnp.float32)
    normed = (
        widened
        * lax.rsqrt(jnp.mean(widened * widened, axis=-1, keepdims=True) + epsilon)
        * norm_gain
    ).astype(jnp.bfloat16)
    tok_rows = routes.shape[0]
    top_count = routes.shape[1]
    local_experts = gate_weight.shape[0]
    owners = lax.axis_size(("seq", "req"))
    experts_all = local_experts * owners
    capacity = min(tok_rows, max(2, 2 * tok_rows * top_count // experts_all))
    flat_ids = routes.reshape(-1)
    flat_count = flat_ids.shape[0]
    match_bool = flat_ids[:, None] == jnp.arange(experts_all, dtype=jnp.int32)[None, :]
    row_pos = jnp.arange(flat_count, dtype=jnp.int32)
    strictly_before = (row_pos[None, :] < row_pos[:, None]).astype(jnp.bfloat16)
    earlier = jnp.dot(
        strictly_before, match_bool.astype(jnp.bfloat16), preferred_element_type=jnp.float32
    )
    slot_rank = jnp.sum(jnp.where(match_bool, earlier, 0.0), axis=1).astype(jnp.int32)
    target = flat_ids * capacity + slot_rank
    slot_ids = jnp.arange(experts_all * capacity, dtype=jnp.int32)
    placing = (target[None, :] == slot_ids[:, None]).astype(jnp.float32)
    token_place = jnp.sum(
        placing.reshape(experts_all * capacity, tok_rows, top_count), axis=-1
    ).astype(jnp.bfloat16)
    outgoing = jnp.dot(token_place, normed, preferred_element_type=jnp.float32).astype(jnp.bfloat16)
    outgoing = outgoing.reshape(owners, local_experts, capacity, -1)
    arrived = lax.all_to_all(outgoing, ("seq", "req"), split_axis=0, concat_axis=0, tiled=True)
    gate_val = jnp.einsum(
        "sjnd,jdf->sjnf", arrived, gate_weight, preferred_element_type=jnp.float32
    )
    upward = jnp.einsum("sjnd,jdf->sjnf", arrived, up_weight, preferred_element_type=jnp.float32)
    activated = (jax.nn.silu(gate_val) * upward).astype(jnp.bfloat16)
    expert_part = jnp.einsum(
        "sjnf,jfd->sjnd", activated, down_weight, preferred_element_type=jnp.float32
    )
    code_float = gate_codes.astype(jnp.float32)
    weights = (code_float / jnp.sum(code_float, axis=-1, keepdims=True)).reshape(-1)
    mixing = jnp.sum(
        (placing * weights[None, :]).reshape(experts_all * capacity, tok_rows, top_count), axis=-1
    ).T
    returned = lax.all_to_all(
        expert_part.astype(jnp.bfloat16), ("seq", "req"), split_axis=0, concat_axis=0, tiled=True
    ).astype(expert_part.dtype)
    mixture = jnp.dot(
        mixing,
        returned.reshape(experts_all * capacity, -1),
        precision=lax.Precision.HIGHEST,
        preferred_element_type=jnp.float32,
    )
    return (widened + mixture).astype(jnp.bfloat16)


def solution(mesh):
    placed = (
        P(("req", "seq", "head"), None),
        P(("req", "seq"), "head"),
        P(("req", "seq"), "head", None, None),
        P(("req", "seq"), "head", None),
        P(("req", "seq"), "head", None),
        P(("req", "seq"), "head", None),
        P("head", "seq"),
        P(),
        P(("req", "seq", "head"), None),
        P(("req", "seq", "head"), None),
        P(("seq", "req"), None, None),
        P(("seq", "req"), None, None),
        P(("seq", "req"), None, None),
    )
    return jax.shard_map(
        on_device,
        mesh=mesh,
        in_specs=placed,
        out_specs=P(("req", "seq", "head"), None),
        check_vma=False,
    )
```

```python
import math

import jax
import jax.numpy as jnp
from jax import lax
from jax.experimental import pallas as pl
from jax.experimental.pallas import tpu as pltpu
from jax.sharding import PartitionSpec as P

epsilon = 1e-06


def find_kept(slots_ref, count_ref, keep):
    segments, requests = count_ref.shape
    listed = slots_ref.shape[0] // segments
    length = keep.shape[1] // segments
    place = lax.broadcasted_iota(jnp.int32, (length, requests), 0)
    for segment in range(segments):
        count = count_ref[segment : segment + 1, :]
        found = jnp.zeros((length, requests), jnp.float32)
        for entry in range(listed):
            at = segment * listed + entry
            slot = jnp.where(entry < count, slots_ref[at : at + 1, :], -1)
            found = jnp.where(place == slot, 1.0, found)
        keep[:, segment * length : (segment + 1) * length] = found.T


def attend_rows(rows_at, first, rows, query_ref, cache_ref, fresh_ref, keep, out_ref, spread, numer):
    context, pair_width = cache_ref.shape[1:]
    width = pair_width // 2
    groups = query_ref.shape[1] // width
    for group in range(groups):
        spread[pl.ds(group, rows, stride=groups), :] = query_ref[
            rows_at, group * width : (group + 1) * width
        ].astype(jnp.float32)
    query = spread[...]
    query_low = query.astype(jnp.bfloat16)
    scores = []
    for pair in range(rows // 2):
        keys = cache_ref[pl.ds(first + 2 * pair, 2), :, :width].reshape(2 * context, width)
        both = lax.dot_general(
            query_low[2 * pair * groups : (2 * pair + 2) * groups, :],
            keys,
            (((1,), (1,)), ((), ())),
            preferred_element_type=jnp.float32,
        )
        scores += [both[:groups, :context], both[groups:, context:]]
    scores = jnp.stack(scores) * width ** (-0.5)
    kept = keep[rows_at, :][:, None, :] > 0.0
    fresh = fresh_ref[rows_at, :].astype(jnp.float32)
    own = (
        jnp.sum(
            query.reshape(rows, groups, width) * fresh[:, None, :width], axis=-1, keepdims=True
        )
        * width ** (-0.5)
    )
    scores = jnp.where(kept, scores, -jnp.inf)
    top = jnp.maximum(jnp.max(scores, axis=-1, keepdims=True), own)
    probs = jnp.exp(scores - top)
    take_new = jnp.exp(own - top)
    denom = jnp.sum(probs, axis=-1, keepdims=True) + take_new
    none = jnp.zeros((groups, context), jnp.float32)
    for pair in range(rows // 2):
        values = cache_ref[pl.ds(first + 2 * pair, 2), :, width:].reshape(2 * context, width)
        upper = jnp.concatenate([probs[2 * pair], none], axis=1)
        lower = jnp.concatenate([none, probs[2 * pair + 1]], axis=1)
        numer[2 * pair * groups : (2 * pair + 2) * groups, :] = jnp.dot(
            jnp.concatenate([upper, lower], axis=0).astype(jnp.bfloat16),
            values,
            preferred_element_type=jnp.float32,
        )
    total = numer[...].reshape(rows, groups, width) + take_new * fresh[:, None, width:]
    numer[...] = (total * (1.0 / denom)).reshape(rows * groups, width)
    for group in range(groups):
        out_ref[:, group * width : (group + 1) * width] = numer[
            pl.ds(group, rows, stride=groups), :
        ].astype(jnp.bfloat16)


def attend_kernel(query_ref, cache_ref, fresh_ref, slots_ref, count_ref, out_ref, keep, spread, numer):
    step = pl.program_id(0)
    rows = cache_ref.shape[0]

    @pl.when(step == 0)
    def _():
        find_kept(slots_ref, count_ref, keep)

    at = pl.ds(pl.multiple_of(step * rows, rows), rows)
    own_keep = keep.at[at]
    attend_rows(
        pl.ds(0, rows), 0, rows, query_ref, cache_ref, fresh_ref, own_keep, out_ref, spread, numer
    )


def attend(queries, cache, fresh, slots, counts):
    requests, context, pair_width = cache.shape
    width = pair_width // 2
    groups = queries.shape[1] // width
    rows = math.gcd(requests, 16)
    return pl.pallas_call(
        attend_kernel,
        grid=(requests // rows,),
        out_shape=jax.ShapeDtypeStruct(queries.shape, jnp.bfloat16),
        in_specs=[
            pl.BlockSpec((rows, queries.shape[1]), lambda i: (i, 0)),
            pl.BlockSpec((rows, context, pair_width), lambda i: (i, 0, 0)),
            pl.BlockSpec((rows, pair_width), lambda i: (i, 0)),
            pl.BlockSpec(slots.shape, lambda i: (0, 0)),
            pl.BlockSpec(counts.shape, lambda i: (0, 0)),
        ],
        out_specs=pl.BlockSpec((rows, queries.shape[1]), lambda i: (i, 0)),
        scratch_shapes=[
            pltpu.VMEM((requests, context), jnp.float32),
            pltpu.VMEM((rows * groups, width), jnp.float32),
            pltpu.VMEM((rows * groups, width), jnp.float32),
        ],
        compiler_params=pltpu.CompilerParams(vmem_limit_bytes=56 * 1024 * 1024),
        cost_estimate=pl.CostEstimate(
            flops=4 * cache.size * groups, bytes_accessed=2 * cache.size, transcendentals=0
        ),
        name="attend",
    )(queries, cache, fresh, slots, counts)


def layer_kernel(
    query_hbm, cache_hbm, fresh_hbm, slots_hbm, count_hbm, outw_hbm, stream_hbm, gain_hbm,
    routes_hbm, codes_hbm, gate_hbm, up_hbm, down_hbm,
    out_ref,
    query_ref, cache_ref, fresh_ref, slots_ref, count_ref, outw, stream_ref, gain_ref,
    routes_ref, codes_ref, gate, up, down,
    keep, spread_rows, numer, heads, gathered, partial, terms, attn, tokens, expert,
    twin_out, twin_in, side_out, side_in,
    load_sem, cache_sem, gather_send, gather_recv, term_send, term_recv, token_send, token_recv,
    twin_send, twin_recv, side_send, side_recv,
):
    head, seq, req = lax.axis_index("head"), lax.axis_index("seq"), lax.axis_index("req")
    head_count, seq_count = lax.axis_size("head"), lax.axis_size("seq")
    tok, model = stream_ref.shape
    columns = outw.shape[1]
    twin = seq + 1 - 2 * (seq % 2)
    far = (seq + 2) % seq_count
    seqs = (seq, twin, far, (twin + 2) % seq_count)
    over_twin, over_far, over_req = {"seq": twin}, {"seq": far}, {"req": 1 - req}

    def load(index, source, target):
        copy = pltpu.make_async_copy(source, target, load_sem.at[index])
        copy.start()
        return copy

    attend_loads = [
        load(0, slots_hbm, slots_ref),
        load(1, count_hbm, count_ref),
        load(2, query_hbm, query_ref),
        load(3, fresh_hbm, fresh_ref),
    ]

    def cache_load(index):
        first = lax.rem(head + 1 + index, head_count) * tok
        rows = pl.ds(pl.multiple_of(first, tok), tok)
        return pltpu.make_async_copy(
            cache_hbm.at[rows], cache_ref.at[rows], cache_sem.at[index]
        )

    for index in range(head_count):
        cache_load(index).start()
    route_loads = [load(4, routes_hbm, routes_ref), load(5, codes_hbm, codes_ref)]
    outw_load = load(6, outw_hbm, outw)
    stream_loads = [load(7, stream_hbm, stream_ref), load(8, gain_hbm, gain_ref)]
    expert_loads = [load(9, gate_hbm, gate), load(10, up_hbm, up), load(11, down_hbm, down)]

    def remote(source, target, sends, recvs, index, device):
        copy = pltpu.make_async_remote_copy(
            src_ref=source,
            dst_ref=target,
            send_sem=sends.at[index],
            recv_sem=recvs.at[index],
            device_id=device,
            device_id_type=pl.DeviceIdType.MESH,
        )
        copy.start()
        return copy

    barrier = pltpu.get_barrier_semaphore()
    corner_at = {"seq": far, "req": 1 - req}
    met = [over_req, corner_at] + [
        {"head": (head + up_by) % head_count, "seq": seqs[k]}
        for up_by in range(head_count)
        for k in range(4)
        if up_by or k
    ]
    for device in met:
        pl.semaphore_signal(barrier, inc=1, device_id=device, device_id_type=pl.DeviceIdType.MESH)

    for copy in attend_loads[:2]:
        copy.wait()
    find_kept(slots_ref, count_ref, keep)
    for copy in attend_loads[2:] + route_loads:
        copy.wait()
    lanes = tokens.shape[2] - model
    number_at = lax.broadcasted_iota(jnp.int32, (lanes, tok), 0)
    coded = jnp.zeros(number_at.shape, jnp.float32)
    for k in range(routes_ref.shape[0]):
        coded = jnp.where(
            routes_ref[k : k + 1, :] == number_at,
            codes_ref[k : k + 1, :].astype(jnp.float32),
            coded,
        )
    tokens[0, :, model:] = coded.T.astype(jnp.bfloat16)

    def attend_group(index, carry):
        cache_load(index).wait()
        first = pl.multiple_of(lax.rem(head + 1 + index, head_count) * tok, tok)
        attend_rows(
            pl.ds(first, tok), first, tok, query_ref, cache_ref, fresh_ref, keep,
            heads.at[index], spread_rows, numer,
        )
        return carry

    sent, summed, to_far, to_twin, passed = [], [], [], [], []

    def project(k, source, part):
        block = source[part].reshape(-1, source.shape[2])
        total = jnp.dot(block, outw[...], preferred_element_type=jnp.float32)
        partial[k, part] = total.astype(jnp.bfloat16).reshape(-1, tok, columns)
        for index in range(part.start, part.stop):
            up_by = (index + 1) % head_count
            if up_by or k:
                summed.append(
                    remote(
                        partial.at[k, index],
                        terms.at[up_by, k],
                        term_send,
                        term_recv,
                        4 * up_by + k,
                        {"head": lax.rem(head + up_by, head_count), "seq": seqs[k]},
                    )
                )

    for i in range(head_count):
        lax.fori_loop(i, i + 1, attend_group, 0)
        if i == 0:
            pl.semaphore_wait(barrier, len(met))
            outw_load.wait()
        to_far.append(
            remote(heads.at[i], gathered.at[1, i], gather_send, gather_recv, i, over_far)
        )
        to_twin.append(
            remote(
                heads.at[i], gathered.at[0, i], gather_send, gather_recv, head_count + i, over_twin
            )
        )
        if i % 2:
            project(0, heads, slice(i - 1, i + 1))

    def pass_on(i):
        to_far[i].wait_recv()
        passed.append(
            remote(
                gathered.at[1, i], gathered.at[2, i], gather_send, gather_recv, 2 * head_count + i,
                over_twin,
            )
        )

    pass_on(0)
    for copy in to_twin:
        copy.wait_recv()
    project(1, gathered.at[0], slice(0, head_count))
    for i in range(1, head_count, 2):
        part = slice(i - 1, i + 1)
        pass_on(i)
        project(2, gathered.at[1], part)
        passed[i - 1].wait_recv()
        passed[i].wait_recv()
        if i + 1 < head_count:
            pass_on(i + 1)
        project(3, gathered.at[2], part)
    sent += to_far + to_twin + passed

    for copy in summed:
        copy.wait_recv()
    for copy in stream_loads:
        copy.wait()
    for k in range(4):
        total = (partial[0, head_count - 1] if k == 0 else terms[0, k]).astype(jnp.float32)
        for up_by in range(1, head_count):
            total = total + terms[up_by, k].astype(jnp.float32)
        attn[:, pl.ds(pl.multiple_of(seqs[k] * columns, columns), columns)] = total
    residual = (stream_ref[...].astype(jnp.float32) + attn[...]).astype(jnp.bfloat16)
    widened = residual.astype(jnp.float32)
    attn[...] = widened
    mean = jnp.mean(widened * widened, axis=-1, keepdims=True)
    tokens[0, :, :model] = (widened * lax.rsqrt(mean + epsilon) * gain_ref[...]).astype(
        jnp.bfloat16
    )

    def spread(source, target, index, device):
        copy = remote(source, target, token_send, token_recv, index, device)
        sent.append(copy)
        return copy

    from_far = spread(tokens.at[0], tokens.at[2], 1, over_far)
    from_req = spread(tokens.at[0], tokens.at[4], 2, over_req)
    from_twin = spread(tokens.at[0], tokens.at[1], 0, over_twin)
    number = seq * lax.axis_size("req") + req

    def hidden(first, count):
        arrived = tokens[first : first + count].reshape(count * tok, tokens.shape[2])
        value = arrived[:, :model]
        codes = arrived[:, model:].astype(jnp.float32)
        place = lax.broadcasted_iota(jnp.int32, codes.shape, 1)
        weight = jnp.sum(jnp.where(place == number, codes, 0.0), axis=-1, keepdims=True) / jnp.sum(
            codes, axis=-1, keepdims=True
        )
        gate_val = jnp.dot(value, gate[...], preferred_element_type=jnp.float32)
        upward = jnp.dot(value, up[...], preferred_element_type=jnp.float32)
        return weight, (jax.nn.silu(gate_val) * upward).astype(jnp.bfloat16)

    def run_expert(first, count):
        weight, act = hidden(first, count)
        value = weight * jnp.dot(act, down[...], preferred_element_type=jnp.float32)
        expert[first * tok : (first + count) * tok, :] = value

    middle = model // 2
    halves = (slice(0, middle), slice(middle, model))

    def to_other_core(slot, side):
        at = 2 * (slot // 2) + side
        value = expert[slot * tok : (slot + 1) * tok, halves[side]]
        twin_out[at] = value.astype(jnp.bfloat16)
        copy = remote(twin_out.at[at], twin_in.at[at], twin_send, twin_recv, at, over_twin)
        sent.append(copy)
        return copy

    def with_other_core(slot, side, copy):
        copy.wait_recv()
        value = expert[slot * tok : (slot + 1) * tok, halves[side]]
        return value + twin_in[2 * (slot // 2) + side].astype(jnp.float32)

    def aside(slot, side, copy, device):
        index = 2 * (slot // 2 - 1) + side
        side_out[index] = with_other_core(slot, side, copy).astype(jnp.bfloat16)
        copy = remote(
            side_out.at[index], side_in.at[index], side_send, side_recv, index, device
        )
        sent.append(copy)
        return copy

    from_twin.wait_recv()
    for copy in expert_loads:
        copy.wait()
    run_expert(0, 2)
    pair = tok // 2
    low, high = pl.ds(0, pair), pl.ds(pair, pair)
    from_far.wait_recv()
    corner = [spread(tokens.at[2, low], tokens.at[6, low], 5, over_req)]
    far_twin = spread(tokens.at[2], tokens.at[3], 3, over_twin)
    from_req.wait_recv()
    corner.append(spread(tokens.at[4, high], tokens.at[6, high], 6, over_far))
    req_twin = spread(tokens.at[4], tokens.at[5], 4, over_twin)
    own_copy = [to_other_core(1, side) for side in range(2)]
    far_twin.wait_recv()
    req_twin.wait_recv()
    run_expert(2, 4)
    far_copy = [to_other_core(3, side) for side in range(2)]
    req_copy = [to_other_core(5, side) for side in range(2)]
    corner_twin = []
    for i, rows in enumerate((low, high)):
        corner[i].wait_recv()
        corner_twin.append(spread(tokens.at[6, rows], tokens.at[7, rows], 7 + i, over_twin))
    landing = [[], []]
    for side in range(2):
        landing[side].append(aside(2, side, far_copy[side], over_far))
        landing[side].append(aside(4, side, req_copy[side], over_req))
    for copy in corner_twin:
        copy.wait_recv()
    weight, act = hidden(6, 2)
    corner_copy = []
    for side in range(2):
        value = jnp.dot(act, down[:, halves[side]], preferred_element_type=jnp.float32)
        expert[6 * tok :, halves[side]] = weight * value
        corner_copy.append(to_other_core(7, side))
    for side in range(2):
        landing[side].append(aside(6, side, corner_copy[side], corner_at))
    for side in range(2):
        total = attn[:, halves[side]] + with_other_core(0, side, own_copy[side])
        for i, copy in enumerate(landing[side]):
            copy.wait_recv()
            total = total + side_in[2 * i + side].astype(jnp.float32)
        out_ref[:, halves[side]] = total.astype(jnp.bfloat16)
    for copy in sent + summed:
        copy.wait_send()


def whole_layer(queries, cache, fresh, slots, counts, outw, stream, gain, routes, codes, gate, up, down):
    tok, model = stream.shape
    requests, context, pair_width = cache.shape
    width = pair_width // 2
    groups = queries.shape[1] // width
    head_count = lax.axis_size("head")
    members = lax.axis_size("seq") * lax.axis_size("req")
    low, dma = jnp.bfloat16, pltpu.SemaphoreType.DMA
    operands = (
        queries, cache, fresh, slots, counts, outw, stream, gain, routes, codes, gate, up, down
    )
    return pl.pallas_call(
        layer_kernel,
        out_shape=jax.ShapeDtypeStruct(stream.shape, stream.dtype),
        in_specs=[pl.BlockSpec(memory_space=pl.ANY)] * len(operands),
        out_specs=pl.BlockSpec(memory_space=pltpu.VMEM),
        scratch_shapes=[
            *[pltpu.VMEM(operand.shape, operand.dtype) for operand in operands],
            pltpu.VMEM((requests, context), jnp.float32),
            pltpu.VMEM((tok * groups, width), jnp.float32),
            pltpu.VMEM((tok * groups, width), jnp.float32),
            pltpu.VMEM((head_count, tok, queries.shape[1]), low),
            pltpu.VMEM((3, head_count, tok, queries.shape[1]), low),
            pltpu.VMEM((4, head_count, tok, outw.shape[1]), low),
            pltpu.VMEM((head_count, 4, tok, outw.shape[1]), low),
            pltpu.VMEM((tok, model), jnp.float32),
            pltpu.VMEM((members, tok, model + 128), low),
            pltpu.VMEM((members * tok, model), jnp.float32),
            pltpu.VMEM((8, tok, model // 2), low),
            pltpu.VMEM((8, tok, model // 2), low),
            pltpu.VMEM((6, tok, model // 2), low),
            pltpu.VMEM((6, tok, model // 2), low),
            dma((12,)),
            dma((head_count,)),
            dma((3 * head_count,)),
            dma((3 * head_count,)),
            dma((4 * head_count,)),
            dma((4 * head_count,)),
            dma((9,)),
            dma((9,)),
            dma((8,)),
            dma((8,)),
            dma((6,)),
            dma((6,)),
        ],
        compiler_params=pltpu.CompilerParams(
            collective_id=0, has_side_effects=True, vmem_limit_bytes=58 * 1024 * 1024
        ),
        name="whole_layer",
    )(*operands)


def on_device(
    stream,
    queries,
    cache_pairs,
    fresh_pairs,
    kept_slots,
    segment_kept_count,
    output_weight,
    norm_gain,
    routes,
    gate_codes,
    gate_weight,
    up_weight,
    down_weight,
):
    req_rows = queries.shape[0]
    cached, fresh = cache_pairs[:, 0], fresh_pairs[:, 0]
    slots, counts = kept_slots[:, 0].T, segment_kept_count[:, 0].T
    experts_all = gate_weight.shape[0] * lax.axis_size(("seq", "req"))
    if (
        lax.axis_size("head") % 2 == 0
        and lax.axis_size("seq") == 4
        and lax.axis_size("req") == 2
        and gate_weight.shape[0] == 1
        and routes.shape[1] == experts_all
        and stream.shape[0] % 32 == 0
        and stream.shape[1] % 256 == 0
    ):
        return whole_layer(
            queries,
            cached,
            fresh,
            slots,
            counts,
            output_weight,
            stream,
            norm_gain[None],
            routes.T,
            gate_codes.T,
            gate_weight[0],
            up_weight[0],
            down_weight[0],
        )
    head_out = attend(queries, cached, fresh, slots, counts)
    partial_value = jnp.dot(
        head_out,
        lax.all_gather(output_weight, "seq", axis=1, tiled=True),
        preferred_element_type=jnp.float32,
    )
    partial_value = partial_value.reshape(1, req_rows, -1)
    summed = lax.psum_scatter(
        partial_value.astype(jnp.bfloat16), "head", scatter_dimension=1, tiled=True
    ).astype(jnp.float32)
    attention = summed.reshape(stream.shape[0], -1)
    residual = (stream.astype(jnp.float32) + attention).astype(jnp.bfloat16)
    widened = residual.astype(jnp.float32)
    normed = (
        widened
        * lax.rsqrt(jnp.mean(widened * widened, axis=-1, keepdims=True) + epsilon)
        * norm_gain
    ).astype(jnp.bfloat16)
    tok_rows = routes.shape[0]
    top_count = routes.shape[1]
    local_experts = gate_weight.shape[0]
    owners = lax.axis_size(("seq", "req"))
    experts_all = local_experts * owners
    capacity = min(tok_rows, max(2, 2 * tok_rows * top_count // experts_all))
    flat_ids = routes.reshape(-1)
    flat_count = flat_ids.shape[0]
    match_bool = flat_ids[:, None] == jnp.arange(experts_all, dtype=jnp.int32)[None, :]
    row_pos = jnp.arange(flat_count, dtype=jnp.int32)
    strictly_before = (row_pos[None, :] < row_pos[:, None]).astype(jnp.bfloat16)
    earlier = jnp.dot(
        strictly_before, match_bool.astype(jnp.bfloat16), preferred_element_type=jnp.float32
    )
    slot_rank = jnp.sum(jnp.where(match_bool, earlier, 0.0), axis=1).astype(jnp.int32)
    target = flat_ids * capacity + slot_rank
    slot_ids = jnp.arange(experts_all * capacity, dtype=jnp.int32)
    placing = (target[None, :] == slot_ids[:, None]).astype(jnp.float32)
    token_place = jnp.sum(
        placing.reshape(experts_all * capacity, tok_rows, top_count), axis=-1
    ).astype(jnp.bfloat16)
    outgoing = jnp.dot(token_place, normed, preferred_element_type=jnp.float32).astype(jnp.bfloat16)
    outgoing = outgoing.reshape(owners, local_experts, capacity, -1)
    arrived = lax.all_to_all(outgoing, ("seq", "req"), split_axis=0, concat_axis=0, tiled=True)
    gate_val = jnp.einsum(
        "sjnd,jdf->sjnf", arrived, gate_weight, preferred_element_type=jnp.float32
    )
    upward = jnp.einsum("sjnd,jdf->sjnf", arrived, up_weight, preferred_element_type=jnp.float32)
    activated = (jax.nn.silu(gate_val) * upward).astype(jnp.bfloat16)
    expert_part = jnp.einsum(
        "sjnf,jfd->sjnd", activated, down_weight, preferred_element_type=jnp.float32
    )
    code_float = gate_codes.astype(jnp.float32)
    weights = (code_float / jnp.sum(code_float, axis=-1, keepdims=True)).reshape(-1)
    mixing = jnp.sum(
        (placing * weights[None, :]).reshape(experts_all * capacity, tok_rows, top_count), axis=-1
    ).T
    returned = lax.all_to_all(
        expert_part.astype(jnp.bfloat16), ("seq", "req"), split_axis=0, concat_axis=0, tiled=True
    ).astype(expert_part.dtype)
    mixture = jnp.dot(
        mixing,
        returned.reshape(experts_all * capacity, -1),
        precision=lax.Precision.HIGHEST,
        preferred_element_type=jnp.float32,
    )
    return (widened + mixture).astype(jnp.bfloat16)


def solution(mesh):
    placed = (
        P(("req", "seq", "head"), None),
        P(("req", "seq"), "head"),
        P(("req", "seq"), "head", None, None),
        P(("req", "seq"), "head", None),
        P(("req", "seq"), "head", None),
        P(("req", "seq"), "head", None),
        P("head", "seq"),
        P(),
        P(("req", "seq", "head"), None),
        P(("req", "seq", "head"), None),
        P(("seq", "req"), None, None),
        P(("seq", "req"), None, None),
        P(("seq", "req"), None, None),
    )
    return jax.shard_map(
        on_device,
        mesh=mesh,
        in_specs=placed,
        out_specs=P(("req", "seq", "head"), None),
        check_vma=False,
    )
```

```python
import math

import jax
import jax.numpy as jnp
from jax import lax
from jax.experimental import pallas as pl
from jax.experimental.pallas import tpu as pltpu
from jax.sharding import PartitionSpec as P

epsilon = 1e-06


def find_kept(slots_ref, count_ref, keep):
    segments, requests = count_ref.shape
    listed = slots_ref.shape[0] // segments
    length = keep.shape[1] // segments
    place = lax.broadcasted_iota(jnp.int32, (length, requests), 0)
    for segment in range(segments):
        count = count_ref[segment : segment + 1, :]
        found = jnp.zeros((length, requests), jnp.float32)
        for entry in range(listed):
            at = segment * listed + entry
            slot = jnp.where(entry < count, slots_ref[at : at + 1, :], -1)
            found = jnp.where(place == slot, 1.0, found)
        keep[:, segment * length : (segment + 1) * length] = found.T


def attend_rows(rows_at, first, rows, query_ref, cache_ref, fresh_ref, keep, out_ref, spread, numer):
    context, pair_width = cache_ref.shape[1:]
    width = pair_width // 2
    groups = query_ref.shape[1] // width
    for group in range(groups):
        spread[pl.ds(group, rows, stride=groups), :] = query_ref[
            rows_at, group * width : (group + 1) * width
        ].astype(jnp.float32)
    query = spread[...]
    query_low = query.astype(jnp.bfloat16)
    scores = []
    for pair in range(rows // 2):
        keys = cache_ref[pl.ds(first + 2 * pair, 2), :, :width].reshape(2 * context, width)
        both = lax.dot_general(
            query_low[2 * pair * groups : (2 * pair + 2) * groups, :],
            keys,
            (((1,), (1,)), ((), ())),
            preferred_element_type=jnp.float32,
        )
        scores += [both[:groups, :context], both[groups:, context:]]
    scores = jnp.stack(scores) * width ** (-0.5)
    kept = keep[rows_at, :][:, None, :] > 0.0
    fresh = fresh_ref[rows_at, :].astype(jnp.float32)
    own = (
        jnp.sum(
            query.reshape(rows, groups, width) * fresh[:, None, :width], axis=-1, keepdims=True
        )
        * width ** (-0.5)
    )
    scores = jnp.where(kept, scores, -jnp.inf)
    top = jnp.maximum(jnp.max(scores, axis=-1, keepdims=True), own)
    probs = jnp.exp(scores - top)
    take_new = jnp.exp(own - top)
    denom = jnp.sum(probs, axis=-1, keepdims=True) + take_new
    none = jnp.zeros((groups, context), jnp.float32)
    for pair in range(rows // 2):
        values = cache_ref[pl.ds(first + 2 * pair, 2), :, width:].reshape(2 * context, width)
        upper = jnp.concatenate([probs[2 * pair], none], axis=1)
        lower = jnp.concatenate([none, probs[2 * pair + 1]], axis=1)
        numer[2 * pair * groups : (2 * pair + 2) * groups, :] = jnp.dot(
            jnp.concatenate([upper, lower], axis=0).astype(jnp.bfloat16),
            values,
            preferred_element_type=jnp.float32,
        )
    total = numer[...].reshape(rows, groups, width) + take_new * fresh[:, None, width:]
    numer[...] = (total * (1.0 / denom)).reshape(rows * groups, width)
    for group in range(groups):
        out_ref[:, group * width : (group + 1) * width] = numer[
            pl.ds(group, rows, stride=groups), :
        ].astype(jnp.bfloat16)


def attend_kernel(query_ref, cache_ref, fresh_ref, slots_ref, count_ref, out_ref, keep, spread, numer):
    step = pl.program_id(0)
    rows = cache_ref.shape[0]

    @pl.when(step == 0)
    def _():
        find_kept(slots_ref, count_ref, keep)

    at = pl.ds(pl.multiple_of(step * rows, rows), rows)
    own_keep = keep.at[at]
    attend_rows(
        pl.ds(0, rows), 0, rows, query_ref, cache_ref, fresh_ref, own_keep, out_ref, spread, numer
    )


def attend(queries, cache, fresh, slots, counts):
    requests, context, pair_width = cache.shape
    width = pair_width // 2
    groups = queries.shape[1] // width
    rows = math.gcd(requests, 16)
    return pl.pallas_call(
        attend_kernel,
        grid=(requests // rows,),
        out_shape=jax.ShapeDtypeStruct(queries.shape, jnp.bfloat16),
        in_specs=[
            pl.BlockSpec((rows, queries.shape[1]), lambda i: (i, 0)),
            pl.BlockSpec((rows, context, pair_width), lambda i: (i, 0, 0)),
            pl.BlockSpec((rows, pair_width), lambda i: (i, 0)),
            pl.BlockSpec(slots.shape, lambda i: (0, 0)),
            pl.BlockSpec(counts.shape, lambda i: (0, 0)),
        ],
        out_specs=pl.BlockSpec((rows, queries.shape[1]), lambda i: (i, 0)),
        scratch_shapes=[
            pltpu.VMEM((requests, context), jnp.float32),
            pltpu.VMEM((rows * groups, width), jnp.float32),
            pltpu.VMEM((rows * groups, width), jnp.float32),
        ],
        compiler_params=pltpu.CompilerParams(vmem_limit_bytes=56 * 1024 * 1024),
        cost_estimate=pl.CostEstimate(
            flops=4 * cache.size * groups, bytes_accessed=2 * cache.size, transcendentals=0
        ),
        name="attend",
    )(queries, cache, fresh, slots, counts)


def layer_kernel(
    query_hbm, cache_hbm, fresh_hbm, slots_hbm, count_hbm, outw_hbm, stream_hbm, gain_hbm,
    routes_hbm, codes_hbm, gate_hbm, up_hbm, down_hbm,
    out_ref,
    query_ref, cache_ref, fresh_ref, slots_ref, count_ref, outw, stream_ref, gain_ref,
    routes_ref, codes_ref, gate, up, down,
    keep, spread_rows, numer, heads, gathered, partial, pairs, pair_sum, terms, attn, tokens, expert,
    twin_out, twin_in, side_out, side_in,
    load_sem, cache_sem, gather_send, gather_recv, pair_send, pair_recv, term_send, term_recv, token_send, token_recv,
    twin_send, twin_recv, side_send, side_recv,
):
    head, seq, req = lax.axis_index("head"), lax.axis_index("seq"), lax.axis_index("req")
    head_count, seq_count = lax.axis_size("head"), lax.axis_size("seq")
    tok, model = stream_ref.shape
    columns = outw.shape[1]
    twin = seq + 1 - 2 * (seq % 2)
    far = (seq + 2) % seq_count
    seqs = (seq, twin, far, (twin + 2) % seq_count)
    beside = head + 1 - 2 * (head % 2)
    beyond = (head + 2) % head_count
    group_of = ((beside + 2) % head_count, beside, beyond, head)
    over_twin, over_far, over_req = {"seq": twin}, {"seq": far}, {"req": 1 - req}

    def load(index, source, target):
        copy = pltpu.make_async_copy(source, target, load_sem.at[index])
        copy.start()
        return copy

    attend_loads = [
        load(0, slots_hbm, slots_ref),
        load(1, count_hbm, count_ref),
        load(2, query_hbm, query_ref),
        load(3, fresh_hbm, fresh_ref),
    ]

    def cache_load(index):
        first = group_of[index] * tok
        rows = pl.ds(pl.multiple_of(first, tok), tok)
        return pltpu.make_async_copy(
            cache_hbm.at[rows], cache_ref.at[rows], cache_sem.at[index]
        )

    for index in range(head_count):
        cache_load(index).start()
    route_loads = [load(4, routes_hbm, routes_ref), load(5, codes_hbm, codes_ref)]
    outw_load = load(6, outw_hbm, outw)
    stream_loads = [load(7, stream_hbm, stream_ref), load(8, gain_hbm, gain_ref)]
    expert_loads = [load(9, gate_hbm, gate), load(10, up_hbm, up), load(11, down_hbm, down)]

    def remote(source, target, sends, recvs, index, device):
        copy = pltpu.make_async_remote_copy(
            src_ref=source,
            dst_ref=target,
            send_sem=sends.at[index],
            recv_sem=recvs.at[index],
            device_id=device,
            device_id_type=pl.DeviceIdType.MESH,
        )
        copy.start()
        return copy

    barrier = pltpu.get_barrier_semaphore()
    corner_at = {"seq": far, "req": 1 - req}
    met = [over_req, corner_at, {"head": beside}]
    met += [{"head": beyond, "seq": seqs[k]} for k in range(4)]
    met += [{"seq": seqs[k]} for k in range(1, 4)]
    for device in met:
        pl.semaphore_signal(barrier, inc=1, device_id=device, device_id_type=pl.DeviceIdType.MESH)

    for copy in attend_loads[:2]:
        copy.wait()
    find_kept(slots_ref, count_ref, keep)
    for copy in attend_loads[2:] + route_loads:
        copy.wait()
    lanes = tokens.shape[2] - model
    number_at = lax.broadcasted_iota(jnp.int32, (lanes, tok), 0)
    coded = jnp.zeros(number_at.shape, jnp.float32)
    for k in range(routes_ref.shape[0]):
        coded = jnp.where(
            routes_ref[k : k + 1, :] == number_at,
            codes_ref[k : k + 1, :].astype(jnp.float32),
            coded,
        )
    tokens[0, :, model:] = coded.T.astype(jnp.bfloat16)

    def attend_group(index):
        cache_load(index).wait()
        first = pl.multiple_of(group_of[index] * tok, tok)
        attend_rows(
            pl.ds(first, tok), first, tok, query_ref, cache_ref, fresh_ref, keep,
            heads.at[index], spread_rows, numer,
        )

    sent, summed, to_far, to_twin, passed, in_pairs = [], [], [], [], [], []

    def project(k, source, part):
        block = source[part].reshape(-1, source.shape[2])
        total = jnp.dot(block, outw[...], preferred_element_type=jnp.float32)
        partial[k, part] = total.astype(jnp.bfloat16).reshape(-1, tok, columns)
        if part.start == 0:
            in_pairs.append(
                remote(
                    partial.at[k, pl.ds(0, 2)],
                    pairs.at[k],
                    pair_send,
                    pair_recv,
                    k,
                    {"head": beside},
                )
            )

    def add_pair(k):
        in_pairs[k].wait_recv()
        total = partial[k, 2:4].astype(jnp.float32) + pairs[k].astype(jnp.float32)
        pair_sum[k] = total.astype(jnp.bfloat16)
        devices = ({"head": beyond, "seq": seqs[k]}, {"seq": seqs[k]})
        for side in range(2 if k else 1):
            summed.append(
                remote(
                    pair_sum.at[k, side],
                    terms.at[side, k],
                    term_send,
                    term_recv,
                    4 * side + k,
                    devices[side],
                )
            )

    for i in range(head_count):
        attend_group(i)
        if i == 0:
            pl.semaphore_wait(barrier, len(met))
            outw_load.wait()
        to_far.append(
            remote(heads.at[i], gathered.at[1, i], gather_send, gather_recv, i, over_far)
        )
        to_twin.append(
            remote(
                heads.at[i], gathered.at[0, i], gather_send, gather_recv, head_count + i, over_twin
            )
        )
        if i % 2:
            project(0, heads, slice(i - 1, i + 1))

    def pass_on(i):
        to_far[i].wait_recv()
        passed.append(
            remote(
                gathered.at[1, i], gathered.at[2, i], gather_send, gather_recv, 2 * head_count + i,
                over_twin,
            )
        )

    pass_on(0)
    for copy in to_twin:
        copy.wait_recv()
    project(1, gathered.at[0], slice(0, head_count))
    early, late = slice(0, 2), slice(2, 4)
    pass_on(1)
    project(2, gathered.at[1], early)
    pass_on(2)
    passed[0].wait_recv()
    passed[1].wait_recv()
    project(3, gathered.at[2], early)
    pass_on(3)
    add_pair(0)
    project(2, gathered.at[1], late)
    add_pair(1)
    passed[2].wait_recv()
    passed[3].wait_recv()
    project(3, gathered.at[2], late)
    add_pair(2)
    add_pair(3)
    sent += in_pairs
    sent += to_far + to_twin + passed

    for copy in summed:
        copy.wait_recv()
    for copy in stream_loads:
        copy.wait()
    for k in range(4):
        total = (terms[1, k] if k else pair_sum[0, 1]).astype(jnp.float32)
        total = total + terms[0, k].astype(jnp.float32)
        attn[:, pl.ds(pl.multiple_of(seqs[k] * columns, columns), columns)] = total
    residual = (stream_ref[...].astype(jnp.float32) + attn[...]).astype(jnp.bfloat16)
    widened = residual.astype(jnp.float32)
    attn[...] = widened
    mean = jnp.mean(widened * widened, axis=-1, keepdims=True)
    tokens[0, :, :model] = (widened * lax.rsqrt(mean + epsilon) * gain_ref[...]).astype(
        jnp.bfloat16
    )

    def spread(source, target, index, device):
        copy = remote(source, target, token_send, token_recv, index, device)
        sent.append(copy)
        return copy

    from_far = spread(tokens.at[0], tokens.at[2], 1, over_far)
    from_req = spread(tokens.at[0], tokens.at[4], 2, over_req)
    from_twin = spread(tokens.at[0], tokens.at[1], 0, over_twin)
    number = seq * lax.axis_size("req") + req

    def hidden(first, count):
        arrived = tokens[first : first + count].reshape(count * tok, tokens.shape[2])
        value = arrived[:, :model]
        codes = arrived[:, model:].astype(jnp.float32)
        place = lax.broadcasted_iota(jnp.int32, codes.shape, 1)
        weight = jnp.sum(jnp.where(place == number, codes, 0.0), axis=-1, keepdims=True) / jnp.sum(
            codes, axis=-1, keepdims=True
        )
        gate_val = jnp.dot(value, gate[...], preferred_element_type=jnp.float32)
        upward = jnp.dot(value, up[...], preferred_element_type=jnp.float32)
        return weight, (jax.nn.silu(gate_val) * upward).astype(jnp.bfloat16)

    def run_expert(first, count):
        weight, act = hidden(first, count)
        value = weight * jnp.dot(act, down[...], preferred_element_type=jnp.float32)
        expert[first * tok : (first + count) * tok, :] = value

    middle = model // 2
    halves = (slice(0, middle), slice(middle, model))

    def to_other_core(slot, side):
        at = 2 * (slot // 2) + side
        value = expert[slot * tok : (slot + 1) * tok, halves[side]]
        twin_out[at] = value.astype(jnp.bfloat16)
        copy = remote(twin_out.at[at], twin_in.at[at], twin_send, twin_recv, at, over_twin)
        sent.append(copy)
        return copy

    def with_other_core(slot, side, copy):
        copy.wait_recv()
        value = expert[slot * tok : (slot + 1) * tok, halves[side]]
        return value + twin_in[2 * (slot // 2) + side].astype(jnp.float32)

    def aside(slot, side, copy, device):
        index = 2 * (slot // 2 - 1) + side
        side_out[index] = with_other_core(slot, side, copy).astype(jnp.bfloat16)
        copy = remote(
            side_out.at[index], side_in.at[index], side_send, side_recv, index, device
        )
        sent.append(copy)
        return copy

    from_twin.wait_recv()
    for copy in expert_loads:
        copy.wait()
    run_expert(0, 2)
    pair = tok // 2
    low, high = pl.ds(0, pair), pl.ds(pair, pair)
    from_far.wait_recv()
    corner = [spread(tokens.at[2, low], tokens.at[6, low], 5, over_req)]
    far_twin = spread(tokens.at[2], tokens.at[3], 3, over_twin)
    from_req.wait_recv()
    corner.append(spread(tokens.at[4, high], tokens.at[6, high], 6, over_far))
    req_twin = spread(tokens.at[4], tokens.at[5], 4, over_twin)
    own_copy = [to_other_core(1, side) for side in range(2)]
    far_twin.wait_recv()
    req_twin.wait_recv()
    run_expert(2, 4)
    far_copy = [to_other_core(3, side) for side in range(2)]
    req_copy = [to_other_core(5, side) for side in range(2)]
    corner_twin = []
    for i, rows in enumerate((low, high)):
        corner[i].wait_recv()
        corner_twin.append(spread(tokens.at[6, rows], tokens.at[7, rows], 7 + i, over_twin))
    landing = [[], []]
    for side in range(2):
        landing[side].append(aside(2, side, far_copy[side], over_far))
        landing[side].append(aside(4, side, req_copy[side], over_req))
    for copy in corner_twin:
        copy.wait_recv()
    weight, act = hidden(6, 2)
    corner_copy = []
    for side in range(2):
        value = jnp.dot(act, down[:, halves[side]], preferred_element_type=jnp.float32)
        expert[6 * tok :, halves[side]] = weight * value
        corner_copy.append(to_other_core(7, side))
    for side in range(2):
        landing[side].append(aside(6, side, corner_copy[side], corner_at))
    for side in range(2):
        total = attn[:, halves[side]] + with_other_core(0, side, own_copy[side])
        for i, copy in enumerate(landing[side]):
            copy.wait_recv()
            total = total + side_in[2 * i + side].astype(jnp.float32)
        out_ref[:, halves[side]] = total.astype(jnp.bfloat16)
    for copy in sent + summed:
        copy.wait_send()


def whole_layer(queries, cache, fresh, slots, counts, outw, stream, gain, routes, codes, gate, up, down):
    tok, model = stream.shape
    requests, context, pair_width = cache.shape
    width = pair_width // 2
    groups = queries.shape[1] // width
    head_count = lax.axis_size("head")
    members = lax.axis_size("seq") * lax.axis_size("req")
    low, dma = jnp.bfloat16, pltpu.SemaphoreType.DMA
    operands = (
        queries, cache, fresh, slots, counts, outw, stream, gain, routes, codes, gate, up, down
    )
    return pl.pallas_call(
        layer_kernel,
        out_shape=jax.ShapeDtypeStruct(stream.shape, stream.dtype),
        in_specs=[pl.BlockSpec(memory_space=pl.ANY)] * len(operands),
        out_specs=pl.BlockSpec(memory_space=pltpu.VMEM),
        scratch_shapes=[
            *[pltpu.VMEM(operand.shape, operand.dtype) for operand in operands],
            pltpu.VMEM((requests, context), jnp.float32),
            pltpu.VMEM((tok * groups, width), jnp.float32),
            pltpu.VMEM((tok * groups, width), jnp.float32),
            pltpu.VMEM((head_count, tok, queries.shape[1]), low),
            pltpu.VMEM((3, head_count, tok, queries.shape[1]), low),
            pltpu.VMEM((4, head_count, tok, outw.shape[1]), low),
            pltpu.VMEM((4, 2, tok, outw.shape[1]), low),
            pltpu.VMEM((4, 2, tok, outw.shape[1]), low),
            pltpu.VMEM((2, 4, tok, outw.shape[1]), low),
            pltpu.VMEM((tok, model), jnp.float32),
            pltpu.VMEM((members, tok, model + 128), low),
            pltpu.VMEM((members * tok, model), jnp.float32),
            pltpu.VMEM((8, tok, model // 2), low),
            pltpu.VMEM((8, tok, model // 2), low),
            pltpu.VMEM((6, tok, model // 2), low),
            pltpu.VMEM((6, tok, model // 2), low),
            dma((12,)),
            dma((head_count,)),
            dma((3 * head_count,)),
            dma((3 * head_count,)),
            dma((4,)),
            dma((4,)),
            dma((8,)),
            dma((8,)),
            dma((9,)),
            dma((9,)),
            dma((8,)),
            dma((8,)),
            dma((6,)),
            dma((6,)),
        ],
        compiler_params=pltpu.CompilerParams(
            collective_id=0, has_side_effects=True, vmem_limit_bytes=58 * 1024 * 1024
        ),
        name="whole_layer",
    )(*operands)


def on_device(
    stream,
    queries,
    cache_pairs,
    fresh_pairs,
    kept_slots,
    segment_kept_count,
    output_weight,
    norm_gain,
    routes,
    gate_codes,
    gate_weight,
    up_weight,
    down_weight,
):
    req_rows = queries.shape[0]
    cached, fresh = cache_pairs[:, 0], fresh_pairs[:, 0]
    slots, counts = kept_slots[:, 0].T, segment_kept_count[:, 0].T
    experts_all = gate_weight.shape[0] * lax.axis_size(("seq", "req"))
    if (
        lax.axis_size("head") == 4
        and lax.axis_size("seq") == 4
        and lax.axis_size("req") == 2
        and gate_weight.shape[0] == 1
        and routes.shape[1] == experts_all
        and stream.shape[0] % 32 == 0
        and stream.shape[1] % 256 == 0
    ):
        return whole_layer(
            queries,
            cached,
            fresh,
            slots,
            counts,
            output_weight,
            stream,
            norm_gain[None],
            routes.T,
            gate_codes.T,
            gate_weight[0],
            up_weight[0],
            down_weight[0],
        )
    head_out = attend(queries, cached, fresh, slots, counts)
    partial_value = jnp.dot(
        head_out,
        lax.all_gather(output_weight, "seq", axis=1, tiled=True),
        preferred_element_type=jnp.float32,
    )
    partial_value = partial_value.reshape(1, req_rows, -1)
    summed = lax.psum_scatter(
        partial_value.astype(jnp.bfloat16), "head", scatter_dimension=1, tiled=True
    ).astype(jnp.float32)
    attention = summed.reshape(stream.shape[0], -1)
    residual = (stream.astype(jnp.float32) + attention).astype(jnp.bfloat16)
    widened = residual.astype(jnp.float32)
    normed = (
        widened
        * lax.rsqrt(jnp.mean(widened * widened, axis=-1, keepdims=True) + epsilon)
        * norm_gain
    ).astype(jnp.bfloat16)
    tok_rows = routes.shape[0]
    top_count = routes.shape[1]
    local_experts = gate_weight.shape[0]
    owners = lax.axis_size(("seq", "req"))
    experts_all = local_experts * owners
    capacity = min(tok_rows, max(2, 2 * tok_rows * top_count // experts_all))
    flat_ids = routes.reshape(-1)
    flat_count = flat_ids.shape[0]
    match_bool = flat_ids[:, None] == jnp.arange(experts_all, dtype=jnp.int32)[None, :]
    row_pos = jnp.arange(flat_count, dtype=jnp.int32)
    strictly_before = (row_pos[None, :] < row_pos[:, None]).astype(jnp.bfloat16)
    earlier = jnp.dot(
        strictly_before, match_bool.astype(jnp.bfloat16), preferred_element_type=jnp.float32
    )
    slot_rank = jnp.sum(jnp.where(match_bool, earlier, 0.0), axis=1).astype(jnp.int32)
    target = flat_ids * capacity + slot_rank
    slot_ids = jnp.arange(experts_all * capacity, dtype=jnp.int32)
    placing = (target[None, :] == slot_ids[:, None]).astype(jnp.float32)
    token_place = jnp.sum(
        placing.reshape(experts_all * capacity, tok_rows, top_count), axis=-1
    ).astype(jnp.bfloat16)
    outgoing = jnp.dot(token_place, normed, preferred_element_type=jnp.float32).astype(jnp.bfloat16)
    outgoing = outgoing.reshape(owners, local_experts, capacity, -1)
    arrived = lax.all_to_all(outgoing, ("seq", "req"), split_axis=0, concat_axis=0, tiled=True)
    gate_val = jnp.einsum(
        "sjnd,jdf->sjnf", arrived, gate_weight, preferred_element_type=jnp.float32
    )
    upward = jnp.einsum("sjnd,jdf->sjnf", arrived, up_weight, preferred_element_type=jnp.float32)
    activated = (jax.nn.silu(gate_val) * upward).astype(jnp.bfloat16)
    expert_part = jnp.einsum(
        "sjnf,jfd->sjnd", activated, down_weight, preferred_element_type=jnp.float32
    )
    code_float = gate_codes.astype(jnp.float32)
    weights = (code_float / jnp.sum(code_float, axis=-1, keepdims=True)).reshape(-1)
    mixing = jnp.sum(
        (placing * weights[None, :]).reshape(experts_all * capacity, tok_rows, top_count), axis=-1
    ).T
    returned = lax.all_to_all(
        expert_part.astype(jnp.bfloat16), ("seq", "req"), split_axis=0, concat_axis=0, tiled=True
    ).astype(expert_part.dtype)
    mixture = jnp.dot(
        mixing,
        returned.reshape(experts_all * capacity, -1),
        precision=lax.Precision.HIGHEST,
        preferred_element_type=jnp.float32,
    )
    return (widened + mixture).astype(jnp.bfloat16)


def solution(mesh):
    placed = (
        P(("req", "seq", "head"), None),
        P(("req", "seq"), "head"),
        P(("req", "seq"), "head", None, None),
        P(("req", "seq"), "head", None),
        P(("req", "seq"), "head", None),
        P(("req", "seq"), "head", None),
        P("head", "seq"),
        P(),
        P(("req", "seq", "head"), None),
        P(("req", "seq", "head"), None),
        P(("seq", "req"), None, None),
        P(("seq", "req"), None, None),
        P(("seq", "req"), None, None),
    )
    return jax.shard_map(
        on_device,
        mesh=mesh,
        in_specs=placed,
        out_specs=P(("req", "seq", "head"), None),
        check_vma=False,
    )
```

```python
import math

import jax
import jax.numpy as jnp
from jax import lax
from jax.experimental import pallas as pl
from jax.experimental.pallas import tpu as pltpu
from jax.sharding import PartitionSpec as P

epsilon = 1e-06


def find_kept(slots_ref, count_ref, keep):
    segments, requests = count_ref.shape
    listed = slots_ref.shape[0] // segments
    length = keep.shape[1] // segments
    place = lax.broadcasted_iota(jnp.int32, (length, requests), 0)
    for segment in range(segments):
        count = count_ref[segment : segment + 1, :]
        found = jnp.zeros((length, requests), jnp.float32)
        for entry in range(listed):
            at = segment * listed + entry
            slot = jnp.where(entry < count, slots_ref[at : at + 1, :], -1)
            found = jnp.where(place == slot, 1.0, found)
        keep[:, segment * length : (segment + 1) * length] = found.T


def attend_rows(rows_at, first, rows, query_ref, cache_ref, fresh_ref, keep, out_ref, spread, numer):
    context, pair_width = cache_ref.shape[1:]
    width = pair_width // 2
    groups = query_ref.shape[1] // width
    for group in range(groups):
        spread[pl.ds(group, rows, stride=groups), :] = query_ref[
            rows_at, group * width : (group + 1) * width
        ].astype(jnp.float32)
    query = spread[...]
    query_low = query.astype(jnp.bfloat16)
    scores = []
    for pair in range(rows // 2):
        keys = cache_ref[pl.ds(first + 2 * pair, 2), :, :width].reshape(2 * context, width)
        both = lax.dot_general(
            query_low[2 * pair * groups : (2 * pair + 2) * groups, :],
            keys,
            (((1,), (1,)), ((), ())),
            preferred_element_type=jnp.float32,
        )
        scores += [both[:groups, :context], both[groups:, context:]]
    scores = jnp.stack(scores) * width ** (-0.5)
    kept = keep[rows_at, :][:, None, :] > 0.0
    fresh = fresh_ref[rows_at, :].astype(jnp.float32)
    own = (
        jnp.sum(
            query.reshape(rows, groups, width) * fresh[:, None, :width], axis=-1, keepdims=True
        )
        * width ** (-0.5)
    )
    scores = jnp.where(kept, scores, -jnp.inf)
    top = jnp.maximum(jnp.max(scores, axis=-1, keepdims=True), own)
    probs = jnp.exp(scores - top)
    take_new = jnp.exp(own - top)
    denom = jnp.sum(probs, axis=-1, keepdims=True) + take_new
    none = jnp.zeros((groups, context), jnp.float32)
    for pair in range(rows // 2):
        values = cache_ref[pl.ds(first + 2 * pair, 2), :, width:].reshape(2 * context, width)
        upper = jnp.concatenate([probs[2 * pair], none], axis=1)
        lower = jnp.concatenate([none, probs[2 * pair + 1]], axis=1)
        numer[2 * pair * groups : (2 * pair + 2) * groups, :] = jnp.dot(
            jnp.concatenate([upper, lower], axis=0).astype(jnp.bfloat16),
            values,
            preferred_element_type=jnp.float32,
        )
    total = numer[...].reshape(rows, groups, width) + take_new * fresh[:, None, width:]
    numer[...] = (total * (1.0 / denom)).reshape(rows * groups, width)
    for group in range(groups):
        out_ref[:, group * width : (group + 1) * width] = numer[
            pl.ds(group, rows, stride=groups), :
        ].astype(jnp.bfloat16)


def attend_kernel(query_ref, cache_ref, fresh_ref, slots_ref, count_ref, out_ref, keep, spread, numer):
    step = pl.program_id(0)
    rows = cache_ref.shape[0]

    @pl.when(step == 0)
    def _():
        find_kept(slots_ref, count_ref, keep)

    at = pl.ds(pl.multiple_of(step * rows, rows), rows)
    own_keep = keep.at[at]
    attend_rows(
        pl.ds(0, rows), 0, rows, query_ref, cache_ref, fresh_ref, own_keep, out_ref, spread, numer
    )


def attend(queries, cache, fresh, slots, counts):
    requests, context, pair_width = cache.shape
    width = pair_width // 2
    groups = queries.shape[1] // width
    rows = math.gcd(requests, 16)
    return pl.pallas_call(
        attend_kernel,
        grid=(requests // rows,),
        out_shape=jax.ShapeDtypeStruct(queries.shape, jnp.bfloat16),
        in_specs=[
            pl.BlockSpec((rows, queries.shape[1]), lambda i: (i, 0)),
            pl.BlockSpec((rows, context, pair_width), lambda i: (i, 0, 0)),
            pl.BlockSpec((rows, pair_width), lambda i: (i, 0)),
            pl.BlockSpec(slots.shape, lambda i: (0, 0)),
            pl.BlockSpec(counts.shape, lambda i: (0, 0)),
        ],
        out_specs=pl.BlockSpec((rows, queries.shape[1]), lambda i: (i, 0)),
        scratch_shapes=[
            pltpu.VMEM((requests, context), jnp.float32),
            pltpu.VMEM((rows * groups, width), jnp.float32),
            pltpu.VMEM((rows * groups, width), jnp.float32),
        ],
        compiler_params=pltpu.CompilerParams(vmem_limit_bytes=56 * 1024 * 1024),
        cost_estimate=pl.CostEstimate(
            flops=4 * cache.size * groups, bytes_accessed=2 * cache.size, transcendentals=0
        ),
        name="attend",
    )(queries, cache, fresh, slots, counts)


def layer_kernel(
    query_hbm, cache_hbm, fresh_hbm, slots_hbm, count_hbm, outw_hbm, stream_hbm, gain_hbm,
    routes_hbm, codes_hbm, gate_hbm, up_hbm, down_hbm,
    out_ref,
    query_ref, cache_ref, fresh_ref, slots_ref, count_ref, outw, stream_ref, gain_ref,
    routes_ref, codes_ref, gate, up, down,
    keep, spread_rows, numer, heads, gathered, partial, terms, attn, tokens, expert,
    twin_out, twin_in, side_out, side_in,
    load_sem, cache_sem, gather_send, gather_recv, term_send, term_recv, token_send, token_recv,
    twin_send, twin_recv, side_send, side_recv,
):
    head, seq, req = lax.axis_index("head"), lax.axis_index("seq"), lax.axis_index("req")
    head_count, seq_count = lax.axis_size("head"), lax.axis_size("seq")
    tok, model = stream_ref.shape
    columns = outw.shape[1]
    twin = seq + 1 - 2 * (seq % 2)
    far = (seq + 2) % seq_count
    seqs = (seq, twin, far, (twin + 2) % seq_count)
    over_twin, over_far, over_req = {"seq": twin}, {"seq": far}, {"req": 1 - req}

    def load(index, source, target):
        copy = pltpu.make_async_copy(source, target, load_sem.at[index])
        copy.start()
        return copy

    attend_loads = [
        load(0, slots_hbm, slots_ref),
        load(1, count_hbm, count_ref),
        load(2, query_hbm, query_ref),
        load(3, fresh_hbm, fresh_ref),
    ]

    def cache_load(index):
        first = lax.rem(head + 1 + index, head_count) * tok
        rows = pl.ds(pl.multiple_of(first, tok), tok)
        return pltpu.make_async_copy(
            cache_hbm.at[rows], cache_ref.at[rows], cache_sem.at[index]
        )

    for index in range(head_count):
        cache_load(index).start()
    route_loads = [load(4, routes_hbm, routes_ref), load(5, codes_hbm, codes_ref)]
    outw_load = load(6, outw_hbm, outw)
    stream_loads = [load(7, stream_hbm, stream_ref), load(8, gain_hbm, gain_ref)]
    expert_loads = [load(9, gate_hbm, gate), load(10, up_hbm, up), load(11, down_hbm, down)]

    def remote(source, target, sends, recvs, index, device):
        copy = pltpu.make_async_remote_copy(
            src_ref=source,
            dst_ref=target,
            send_sem=sends.at[index],
            recv_sem=recvs.at[index],
            device_id=device,
            device_id_type=pl.DeviceIdType.MESH,
        )
        copy.start()
        return copy

    barrier = pltpu.get_barrier_semaphore()
    corner_at = {"seq": far, "req": 1 - req}
    met = [over_req, corner_at] + [
        {"head": (head + up_by) % head_count, "seq": seqs[k]}
        for up_by in range(head_count)
        for k in range(4)
        if up_by or k
    ]
    for device in met:
        pl.semaphore_signal(barrier, inc=1, device_id=device, device_id_type=pl.DeviceIdType.MESH)

    for copy in attend_loads[:2]:
        copy.wait()
    find_kept(slots_ref, count_ref, keep)
    for copy in attend_loads[2:] + route_loads:
        copy.wait()
    lanes = tokens.shape[2] - model
    number_at = lax.broadcasted_iota(jnp.int32, (lanes, tok), 0)
    coded = jnp.zeros(number_at.shape, jnp.float32)
    for k in range(routes_ref.shape[0]):
        coded = jnp.where(
            routes_ref[k : k + 1, :] == number_at,
            codes_ref[k : k + 1, :].astype(jnp.float32),
            coded,
        )
    tokens[0, :, model:] = coded.T.astype(jnp.bfloat16)

    def attend_group(index, carry):
        cache_load(index).wait()
        first = pl.multiple_of(lax.rem(head + 1 + index, head_count) * tok, tok)
        attend_rows(
            pl.ds(first, tok), first, tok, query_ref, cache_ref, fresh_ref, keep,
            heads.at[index], spread_rows, numer,
        )
        return carry

    sent, summed, to_far, to_twin, passed = [], [], [], [], []

    def project(k, source, part):
        block = source[part].reshape(-1, source.shape[2])
        total = jnp.dot(block, outw[...], preferred_element_type=jnp.float32)
        partial[k, part] = total.astype(jnp.bfloat16).reshape(-1, tok, columns)
        for index in range(part.start, part.stop):
            up_by = (index + 1) % head_count
            if up_by or k:
                summed.append(
                    remote(
                        partial.at[k, index],
                        terms.at[up_by, k],
                        term_send,
                        term_recv,
                        4 * up_by + k,
                        {"head": lax.rem(head + up_by, head_count), "seq": seqs[k]},
                    )
                )

    for i in range(head_count):
        lax.fori_loop(i, i + 1, attend_group, 0)
        if i == 0:
            pl.semaphore_wait(barrier, len(met))
            outw_load.wait()
        to_far.append(
            remote(heads.at[i], gathered.at[1, i], gather_send, gather_recv, i, over_far)
        )
        to_twin.append(
            remote(
                heads.at[i], gathered.at[0, i], gather_send, gather_recv, head_count + i, over_twin
            )
        )
        if i % 2:
            project(0, heads, slice(i - 1, i + 1))

    def pass_on(i):
        to_far[i].wait_recv()
        passed.append(
            remote(
                gathered.at[1, i], gathered.at[2, i], gather_send, gather_recv, 2 * head_count + i,
                over_twin,
            )
        )

    early, late = slice(0, head_count // 2), slice(head_count // 2, head_count)
    for i in range(early.start, early.stop):
        pass_on(i)
    for copy in to_twin:
        copy.wait_recv()
    project(1, gathered.at[0], slice(0, head_count))
    project(2, gathered.at[1], early)
    for i in range(late.start, late.stop):
        pass_on(i)
    for i in range(early.start, early.stop):
        passed[i].wait_recv()
    project(3, gathered.at[2], early)
    project(2, gathered.at[1], late)
    for i in range(late.start, late.stop):
        passed[i].wait_recv()
    project(3, gathered.at[2], late)
    sent += to_far + to_twin + passed

    for copy in summed:
        copy.wait_recv()
    for copy in stream_loads:
        copy.wait()
    for k in range(4):
        total = (partial[0, head_count - 1] if k == 0 else terms[0, k]).astype(jnp.float32)
        for up_by in range(1, head_count):
            total = total + terms[up_by, k].astype(jnp.float32)
        attn[:, pl.ds(pl.multiple_of(seqs[k] * columns, columns), columns)] = total
    residual = (stream_ref[...].astype(jnp.float32) + attn[...]).astype(jnp.bfloat16)
    widened = residual.astype(jnp.float32)
    attn[...] = widened
    mean = jnp.mean(widened * widened, axis=-1, keepdims=True)
    tokens[0, :, :model] = (widened * lax.rsqrt(mean + epsilon) * gain_ref[...]).astype(
        jnp.bfloat16
    )

    def spread(source, target, index, device):
        copy = remote(source, target, token_send, token_recv, index, device)
        sent.append(copy)
        return copy

    from_far = spread(tokens.at[0], tokens.at[2], 1, over_far)
    from_req = spread(tokens.at[0], tokens.at[4], 2, over_req)
    from_twin = spread(tokens.at[0], tokens.at[1], 0, over_twin)
    from_corner = spread(tokens.at[0], tokens.at[6], 5, corner_at)
    number = seq * lax.axis_size("req") + req

    def hidden(first, count):
        arrived = tokens[first : first + count].reshape(count * tok, tokens.shape[2])
        value = arrived[:, :model]
        codes = arrived[:, model:].astype(jnp.float32)
        place = lax.broadcasted_iota(jnp.int32, codes.shape, 1)
        weight = jnp.sum(jnp.where(place == number, codes, 0.0), axis=-1, keepdims=True) / jnp.sum(
            codes, axis=-1, keepdims=True
        )
        gate_val = jnp.dot(value, gate[...], preferred_element_type=jnp.float32)
        upward = jnp.dot(value, up[...], preferred_element_type=jnp.float32)
        return weight, (jax.nn.silu(gate_val) * upward).astype(jnp.bfloat16)

    def lower(first, count, weight, act):
        value = weight * jnp.dot(act, down[...], preferred_element_type=jnp.float32)
        expert[first * tok : (first + count) * tok, :] = value

    middle = model // 2
    halves = (slice(0, middle), slice(middle, model))

    def to_other_core(slot, side):
        at = 2 * (slot // 2) + side
        value = expert[slot * tok : (slot + 1) * tok, halves[side]]
        twin_out[at] = value.astype(jnp.bfloat16)
        copy = remote(twin_out.at[at], twin_in.at[at], twin_send, twin_recv, at, over_twin)
        sent.append(copy)
        return copy

    def with_other_core(slot, side, copy):
        copy.wait_recv()
        value = expert[slot * tok : (slot + 1) * tok, halves[side]]
        return value + twin_in[2 * (slot // 2) + side].astype(jnp.float32)

    def aside(slot, side, copy, device):
        index = 2 * (slot // 2 - 1) + side
        side_out[index] = with_other_core(slot, side, copy).astype(jnp.bfloat16)
        copy = remote(
            side_out.at[index], side_in.at[index], side_send, side_recv, index, device
        )
        sent.append(copy)
        return copy

    from_twin.wait_recv()
    for copy in expert_loads:
        copy.wait()
    lower(0, 2, *hidden(0, 2))
    from_far.wait_recv()
    far_twin = spread(tokens.at[2], tokens.at[3], 3, over_twin)
    from_req.wait_recv()
    req_twin = spread(tokens.at[4], tokens.at[5], 4, over_twin)
    own_copy = [to_other_core(1, side) for side in range(2)]
    far_twin.wait_recv()
    req_twin.wait_recv()
    weight, act = hidden(2, 4)
    from_corner.wait_recv()
    corner_twin = spread(tokens.at[6], tokens.at[7], 6, over_twin)
    lower(2, 4, weight, act)
    far_copy = [to_other_core(3, side) for side in range(2)]
    req_copy = [to_other_core(5, side) for side in range(2)]
    landing = [[], []]
    for side in range(2):
        landing[side].append(aside(2, side, far_copy[side], over_far))
        landing[side].append(aside(4, side, req_copy[side], over_req))
    corner_twin.wait_recv()
    weight, act = hidden(6, 2)
    corner_copy = []
    for side in range(2):
        value = jnp.dot(act, down[:, halves[side]], preferred_element_type=jnp.float32)
        expert[6 * tok :, halves[side]] = weight * value
        corner_copy.append(to_other_core(7, side))
    for side in range(2):
        landing[side].append(aside(6, side, corner_copy[side], corner_at))
    for side in range(2):
        total = attn[:, halves[side]] + with_other_core(0, side, own_copy[side])
        for i, copy in enumerate(landing[side]):
            copy.wait_recv()
            total = total + side_in[2 * i + side].astype(jnp.float32)
        out_ref[:, halves[side]] = total.astype(jnp.bfloat16)
    for copy in sent + summed:
        copy.wait_send()


def whole_layer(queries, cache, fresh, slots, counts, outw, stream, gain, routes, codes, gate, up, down):
    tok, model = stream.shape
    requests, context, pair_width = cache.shape
    width = pair_width // 2
    groups = queries.shape[1] // width
    head_count = lax.axis_size("head")
    members = lax.axis_size("seq") * lax.axis_size("req")
    low, dma = jnp.bfloat16, pltpu.SemaphoreType.DMA
    operands = (
        queries, cache, fresh, slots, counts, outw, stream, gain, routes, codes, gate, up, down
    )
    return pl.pallas_call(
        layer_kernel,
        out_shape=jax.ShapeDtypeStruct(stream.shape, stream.dtype),
        in_specs=[pl.BlockSpec(memory_space=pl.ANY)] * len(operands),
        out_specs=pl.BlockSpec(memory_space=pltpu.VMEM),
        scratch_shapes=[
            *[pltpu.VMEM(operand.shape, operand.dtype) for operand in operands],
            pltpu.VMEM((requests, context), jnp.float32),
            pltpu.VMEM((tok * groups, width), jnp.float32),
            pltpu.VMEM((tok * groups, width), jnp.float32),
            pltpu.VMEM((head_count, tok, queries.shape[1]), low),
            pltpu.VMEM((3, head_count, tok, queries.shape[1]), low),
            pltpu.VMEM((4, head_count, tok, outw.shape[1]), low),
            pltpu.VMEM((head_count, 4, tok, outw.shape[1]), low),
            pltpu.VMEM((tok, model), jnp.float32),
            pltpu.VMEM((members, tok, model + 128), low),
            pltpu.VMEM((members * tok, model), jnp.float32),
            pltpu.VMEM((8, tok, model // 2), low),
            pltpu.VMEM((8, tok, model // 2), low),
            pltpu.VMEM((6, tok, model // 2), low),
            pltpu.VMEM((6, tok, model // 2), low),
            dma((12,)),
            dma((head_count,)),
            dma((3 * head_count,)),
            dma((3 * head_count,)),
            dma((4 * head_count,)),
            dma((4 * head_count,)),
            dma((7,)),
            dma((7,)),
            dma((8,)),
            dma((8,)),
            dma((6,)),
            dma((6,)),
        ],
        compiler_params=pltpu.CompilerParams(
            collective_id=0, has_side_effects=True, vmem_limit_bytes=58 * 1024 * 1024
        ),
        name="whole_layer",
    )(*operands)


def on_device(
    stream,
    queries,
    cache_pairs,
    fresh_pairs,
    kept_slots,
    segment_kept_count,
    output_weight,
    norm_gain,
    routes,
    gate_codes,
    gate_weight,
    up_weight,
    down_weight,
):
    req_rows = queries.shape[0]
    cached, fresh = cache_pairs[:, 0], fresh_pairs[:, 0]
    slots, counts = kept_slots[:, 0].T, segment_kept_count[:, 0].T
    experts_all = gate_weight.shape[0] * lax.axis_size(("seq", "req"))
    if (
        lax.axis_size("head") % 2 == 0
        and lax.axis_size("seq") == 4
        and lax.axis_size("req") == 2
        and gate_weight.shape[0] == 1
        and routes.shape[1] == experts_all
        and stream.shape[0] % 32 == 0
        and stream.shape[1] % 256 == 0
    ):
        return whole_layer(
            queries,
            cached,
            fresh,
            slots,
            counts,
            output_weight,
            stream,
            norm_gain[None],
            routes.T,
            gate_codes.T,
            gate_weight[0],
            up_weight[0],
            down_weight[0],
        )
    head_out = attend(queries, cached, fresh, slots, counts)
    partial_value = jnp.dot(
        head_out,
        lax.all_gather(output_weight, "seq", axis=1, tiled=True),
        preferred_element_type=jnp.float32,
    )
    partial_value = partial_value.reshape(1, req_rows, -1)
    summed = lax.psum_scatter(
        partial_value.astype(jnp.bfloat16), "head", scatter_dimension=1, tiled=True
    ).astype(jnp.float32)
    attention = summed.reshape(stream.shape[0], -1)
    residual = (stream.astype(jnp.float32) + attention).astype(jnp.bfloat16)
    widened = residual.astype(jnp.float32)
    normed = (
        widened
        * lax.rsqrt(jnp.mean(widened * widened, axis=-1, keepdims=True) + epsilon)
        * norm_gain
    ).astype(jnp.bfloat16)
    tok_rows = routes.shape[0]
    top_count = routes.shape[1]
    local_experts = gate_weight.shape[0]
    owners = lax.axis_size(("seq", "req"))
    experts_all = local_experts * owners
    capacity = min(tok_rows, max(2, 2 * tok_rows * top_count // experts_all))
    flat_ids = routes.reshape(-1)
    flat_count = flat_ids.shape[0]
    match_bool = flat_ids[:, None] == jnp.arange(experts_all, dtype=jnp.int32)[None, :]
    row_pos = jnp.arange(flat_count, dtype=jnp.int32)
    strictly_before = (row_pos[None, :] < row_pos[:, None]).astype(jnp.bfloat16)
    earlier = jnp.dot(
        strictly_before, match_bool.astype(jnp.bfloat16), preferred_element_type=jnp.float32
    )
    slot_rank = jnp.sum(jnp.where(match_bool, earlier, 0.0), axis=1).astype(jnp.int32)
    target = flat_ids * capacity + slot_rank
    slot_ids = jnp.arange(experts_all * capacity, dtype=jnp.int32)
    placing = (target[None, :] == slot_ids[:, None]).astype(jnp.float32)
    token_place = jnp.sum(
        placing.reshape(experts_all * capacity, tok_rows, top_count), axis=-1
    ).astype(jnp.bfloat16)
    outgoing = jnp.dot(token_place, normed, preferred_element_type=jnp.float32).astype(jnp.bfloat16)
    outgoing = outgoing.reshape(owners, local_experts, capacity, -1)
    arrived = lax.all_to_all(outgoing, ("seq", "req"), split_axis=0, concat_axis=0, tiled=True)
    gate_val = jnp.einsum(
        "sjnd,jdf->sjnf", arrived, gate_weight, preferred_element_type=jnp.float32
    )
    upward = jnp.einsum("sjnd,jdf->sjnf", arrived, up_weight, preferred_element_type=jnp.float32)
    activated = (jax.nn.silu(gate_val) * upward).astype(jnp.bfloat16)
    expert_part = jnp.einsum(
        "sjnf,jfd->sjnd", activated, down_weight, preferred_element_type=jnp.float32
    )
    code_float = gate_codes.astype(jnp.float32)
    weights = (code_float / jnp.sum(code_float, axis=-1, keepdims=True)).reshape(-1)
    mixing = jnp.sum(
        (placing * weights[None, :]).reshape(experts_all * capacity, tok_rows, top_count), axis=-1
    ).T
    returned = lax.all_to_all(
        expert_part.astype(jnp.bfloat16), ("seq", "req"), split_axis=0, concat_axis=0, tiled=True
    ).astype(expert_part.dtype)
    mixture = jnp.dot(
        mixing,
        returned.reshape(experts_all * capacity, -1),
        precision=lax.Precision.HIGHEST,
        preferred_element_type=jnp.float32,
    )
    return (widened + mixture).astype(jnp.bfloat16)


def solution(mesh):
    placed = (
        P(("req", "seq", "head"), None),
        P(("req", "seq"), "head"),
        P(("req", "seq"), "head", None, None),
        P(("req", "seq"), "head", None),
        P(("req", "seq"), "head", None),
        P(("req", "seq"), "head", None),
        P("head", "seq"),
        P(),
        P(("req", "seq", "head"), None),
        P(("req", "seq", "head"), None),
        P(("seq", "req"), None, None),
        P(("seq", "req"), None, None),
        P(("seq", "req"), None, None),
    )
    return jax.shard_map(
        on_device,
        mesh=mesh,
        in_specs=placed,
        out_specs=P(("req", "seq", "head"), None),
        check_vma=False,
    )
```
